512 devices in a mesh: rep: 16 (over y_lo, z), tok: 32 (over x, y_hi, core).
Axes of the slice: x: 4, y: 8 (y_hi: 4, y_lo: 2; y = y_hi * 2 + y_lo), z: 8, core: 2. Of those that a mesh axis runs over, the one named last changes fastest.
Arguments:
- query_rows: bfloat16 [16, 4096, 1024], P('rep', 'tok'), may hold values from -144 to 144
- key_rows: bfloat16 [16, 4096, 1024], P('rep', 'tok'), may hold values from -7 to 7
- value_rows: bfloat16 [16, 4096, 1024], P('rep', 'tok'), may hold values from -6 to 6
- cotangent: bfloat16 [16, 4096, 1024], P('rep', 'tok'), may hold values from -6 to 6
- out_weight: bfloat16 [1024, 1024], replicated, may hold values from -0.1875 to 0.1875
- error_rows: float32 [16, 1024, 1024], P('rep', 'tok'), may hold values from -4 to 4
- window_shift: int32 [16], P('rep'), may hold values from 0 to 127
- basis_seed: int32 [1], replicated, may hold values from 0 to 999
Outputs:
- projected: bfloat16 [16, 4096, 1024], P('rep', 'tok')
- query_grad: bfloat16 [16, 4096, 1024], P('rep', 'tok')
- key_grad: bfloat16 [16, 4096, 1024], P('rep', 'tok')
- value_grad: bfloat16 [16, 4096, 1024], P('rep', 'tok')
- weight_update: float32 [1024, 1024], P('tok')
- new_error: float32 [16, 1024, 1024], P('rep', 'tok')
- new_basis: float32 [1024, 32], replicated
The draws below stay inside these ranges and needn't reach their ends.
All inputs are finite; a program needn't handle non-finite values.
Results may differ from the reference program's by a relative error of at most 0.007.
Values may be sent and summed in bfloat16 or wider, within the bound.
A program may use at most 128 MiB of HBM per device.

```python
import math
import jax
import jax.numpy as jnp
from jax import lax

D = 1024
H = 16
HD = 64
WIN = 128
RANK = 32
TOKENS = 4096
SAMPLES = 16


def key_field(key):
    base = jax.random.normal(jax.random.fold_in(key, 11), (SAMPLES, TOKENS, D), jnp.float32)
    return jnp.clip(base, -6.0, 6.0)


def draw_key_rows(key, part):
    base = key_field(key)
    return base.astype(jnp.bfloat16)


def draw_query_rows(key, part):
    key = jax.random.fold_in(key, 5)
    own = jnp.clip(jax.random.normal(key, (SAMPLES, TOKENS, D), jnp.float32), -6.0, 6.0)
    return own.astype(jnp.bfloat16)


def touch_ends(values, rng, low, largest):
    dims = values.shape
    place = [jax.random.randint(jax.random.fold_in(rng, axis), (), 0, dims[axis]) for axis in range(len(dims))]
    values = values.at[tuple(place)].set(low)
    longest = dims.index(max(dims))
    place[longest] = (place[longest] + 1) % dims[longest]
    return values.at[tuple(place)].set(largest)


def steps_of(key, dims, pieces, least, largest):
    level = 1.0
    for dim, shards_of in pieces:
        draws = jax.random.uniform(jax.random.fold_in(jax.random.fold_in(key, 6), dim), (shards_of,), jnp.float32, least / len(pieces), largest / len(pieces))
        level = level * jnp.repeat(jnp.exp(draws), dims[dim] // shards_of).reshape((-1,) + (1,) * (len(dims) - 1 - dim))
    return level


def scatter_about(rng, extent, width, limit, cuts=(), kind=jnp.bfloat16):
    gain = steps_of(rng, extent, cuts, -0.22, 0.18) if cuts else 1.0
    entries = jax.random.normal(rng, extent, jnp.float32) * width * gain
    return jnp.minimum(jnp.maximum(entries, -limit), limit).astype(kind)


def setup_inputs(seed: int = 0) -> dict:
    arg_keys = jax.random.split(jax.random.key(seed), 9)
    return {
        "query_rows": draw_query_rows(jax.random.fold_in(arg_keys[8], 71), 0),
        "key_rows": draw_key_rows(jax.random.fold_in(arg_keys[8], 71), 0),
        "value_rows": scatter_about(arg_keys[2], (SAMPLES, TOKENS, D), 1.0, 6.0, ((0, 16), (1, 32))),
        "cotangent": scatter_about(arg_keys[3], (SAMPLES, TOKENS, D), 1.0, 6.0, ((0, 16), (1, 32))),
        "out_weight": scatter_about(arg_keys[4], (D, D), D ** -0.5, 0.1875),
        "error_rows": scatter_about(arg_keys[5], (SAMPLES, D, D), 0.5, 4.0, ((0, 16), (1, 32)), jnp.float32),
        "window_shift": touch_ends(jax.random.randint(arg_keys[6], (SAMPLES,), 0, WIN), jax.random.fold_in(arg_keys[6], 1), 0, WIN - 1).astype(jnp.int32),
        "basis_seed": jax.random.randint(arg_keys[7], (1,), 0, 1000).astype(jnp.int32),
    }


def seeded_basis(seed_value, row_count, col_count):
    row_index = jnp.arange(row_count, dtype=jnp.int32)[:, None]
    col_index = jnp.arange(col_count, dtype=jnp.int32)[None, :]
    mixed = (row_index * 7919 + col_index * 31337 + seed_value * 17 + 12345) % 65521
    mixed = (mixed * 3877 + 29) % 65521
    mixed = (mixed * 2011 + 7) % 65521
    return mixed.astype(jnp.float32) / 65521.0 - 0.5

def one_sample(inputs, out_weight):
    query, keyed, valued, upstream, shift = inputs
    scale_factor = 1.0 / math.sqrt(HD)
    count = TOKENS // WIN

    def to_windows(field):
        return jnp.roll(field, -shift, axis=0).reshape(count, WIN, H, HD).astype(jnp.float32)

    def from_windows(field):
        return jnp.roll(field.reshape(TOKENS, D), shift, axis=0)
    query_w = to_windows(query)
    key_w = to_windows(keyed)
    value_w = to_windows(valued)
    scores = jnp.einsum('wqhd,wkhd->whqk', query_w, key_w) * scale_factor
    top = lax.optimization_barrier(jnp.max(scores, axis=-1, keepdims=True))
    expo = jnp.exp(scores - top)
    probs = expo / lax.optimization_barrier(jnp.sum(expo, axis=-1, keepdims=True))
    probs_low = probs.astype(jnp.bfloat16)
    attn_w = jnp.einsum('whqk,wkhd->wqhd', probs_low.astype(jnp.float32), value_w).astype(jnp.bfloat16)
    attn = from_windows(attn_w)
    projected = jnp.dot(attn.astype(jnp.float32), out_weight.astype(jnp.float32), preferred_element_type=jnp.float32).astype(jnp.bfloat16)
    dattn = jnp.dot(upstream.astype(jnp.float32), out_weight.T.astype(jnp.float32), preferred_element_type=jnp.float32).astype(jnp.bfloat16)
    dattn_w = to_windows(dattn)
    dprob = jnp.einsum('wqhd,wkhd->whqk', dattn_w, value_w)
    delta = lax.optimization_barrier(jnp.sum(probs * dprob, axis=-1, keepdims=True))
    dscore = (probs * (dprob - delta) * scale_factor).astype(jnp.bfloat16).astype(jnp.float32)
    query_grad = from_windows(jnp.einsum('whqk,wkhd->wqhd', dscore, key_w).astype(jnp.bfloat16))
    key_grad = from_windows(jnp.einsum('whqk,wqhd->wkhd', dscore, query_w).astype(jnp.bfloat16))
    value_grad = from_windows(jnp.einsum('whqk,wqhd->wkhd', probs_low.astype(jnp.float32), dattn_w).astype(jnp.bfloat16))
    grad = jnp.dot(attn.T.astype(jnp.float32), upstream.astype(jnp.float32), preferred_element_type=jnp.float32) * (1.0 / math.sqrt(TOKENS))
    return (projected, query_grad, key_grad, value_grad, grad)

def reference(query_rows, key_rows, value_rows, cotangent, out_weight, error_rows, window_shift, basis_seed):
    projected, query_grad, key_grad, value_grad, grad = lax.map(lambda inputs: one_sample(inputs, out_weight), (query_rows, key_rows, value_rows, cotangent, window_shift))
    merged = grad + error_rows
    basis = seeded_basis(basis_seed[0], D, RANK)
    highest = lax.Precision.HIGHEST
    left = jnp.einsum('rij,jc->ic', merged, basis, precision=highest) / SAMPLES
    gram = jnp.dot(left.T, left, precision=highest)
    lower = jnp.linalg.cholesky(gram)
    ortho = lax.linalg.triangular_solve(lower, left, left_side=False, lower=True, transpose_a=True)
    new_basis = jnp.einsum('rij,ic->jc', merged, ortho, precision=highest) / SAMPLES
    weight_update = jnp.dot(ortho, new_basis.T, precision=highest)
    new_error = merged - weight_update[None]
    return (projected, query_grad, key_grad, value_grad, weight_update, new_error, new_basis)
```

```python
import math

import jax
import jax.numpy as jnp
from jax import lax
from jax.experimental import pallas as pl
from jax.experimental.pallas import tpu as pltpu
from jax.sharding import PartitionSpec as P

H = 16
HD = 64
WIN = 128
HALF = 64
RANK = 32
WIDTH = 1024
TOK = 32
REP = 16
GRAD_SCALE = 1.0 / 64.0
F32 = jnp.float32
BF16 = jnp.bfloat16
MESH = pl.DeviceIdType.MESH
HIGHEST = lax.Precision.HIGHEST
NN = (((1,), (0,)), ((), ()))
NT = (((1,), (1,)), ((), ()))
TN = (((0,), (0,)), ((), ()))


def seeded_basis_t(seed_value):
    row_index = jnp.arange(WIDTH, dtype=jnp.int32)[None, :]
    col_index = jnp.arange(RANK, dtype=jnp.int32)[:, None]
    mixed = (row_index * 7919 + col_index * 31337 + seed_value * 17 + 12345) % 65521
    mixed = (mixed * 3877 + 29) % 65521
    mixed = (mixed * 2011 + 7) % 65521
    return mixed.astype(F32) / 65521.0 - 0.5


def mm(a, b, dims=NN):
    return lax.dot_general(a, b, dims, preferred_element_type=F32)


def mm_exact(a, b, dims=NN):
    return lax.dot_general(a, b, dims, precision=HIGHEST, preferred_element_type=F32)


def mm_split(a, b, dims=NN):
    high = a.astype(BF16)
    rest = a - high.astype(F32)
    middle = rest.astype(BF16)
    low = (rest - middle.astype(F32)).astype(BF16)
    out = mm(jnp.concatenate([high, middle, low], 0), b, dims)
    return (out[2 * RANK :] + out[RANK : 2 * RANK]) + out[:RANK]


def one_hot(shape, row_to_col):
    rows = lax.broadcasted_iota(jnp.int32, shape, 0)
    cols = lax.broadcasted_iota(jnp.int32, shape, 1)
    return jnp.where(row_to_col(rows, cols), 1.0, 0.0).astype(BF16)


def to_tiles(ref, field):
    for i in range(4):
        for j in range(8):
            ref[i * 8 + j] = field[i * 8 : i * 8 + 8, j * 128 : j * 128 + 128]


def attend_kernel(
    shift, query, key, value, cot, weight, basis, error,
    outs, grad, left, attn_out, cot_out,
    cat, weight_v, win, dattn, proj, send_sem, recv_sem, local_sem,
):
    me = lax.axis_index("tok")
    next_dev, prev_dev = lax.rem(me + 1, TOK), lax.rem(me + TOK - 1, TOK)
    barrier = pltpu.get_barrier_semaphore()
    for dev in (next_dev, prev_dev):
        pl.semaphore_signal(barrier, inc=1, device_id={"tok": dev}, device_id_type=MESH)
    local = []
    sources = (cot, key, query, value)
    for i, src in enumerate(sources):
        local.append(pltpu.make_async_copy(src, cat.at[i, pl.ds(HALF, WIN)], local_sem.at[i]))
    local.append(pltpu.make_async_copy(weight, weight_v, local_sem.at[4]))
    for copy in local:
        copy.start()
    pl.semaphore_wait(barrier, 2)
    halo = []
    for i, src in enumerate(sources):
        halo.append(
            pltpu.make_async_remote_copy(
                src.at[pl.ds(0, HALF)], cat.at[i, pl.ds(HALF + WIN, HALF)],
                send_sem.at[2 * i], recv_sem.at[2 * i],
                device_id={"tok": prev_dev}, device_id_type=MESH,
            )
        )
        halo.append(
            pltpu.make_async_remote_copy(
                src.at[pl.ds(HALF, HALF)], cat.at[i, pl.ds(0, HALF)],
                send_sem.at[2 * i + 1], recv_sem.at[2 * i + 1],
                device_id={"tok": next_dev}, device_id_type=MESH,
            )
        )
    for copy in halo:
        copy.start()
    for copy in local:
        copy.wait()

    offset = shift[0]
    start = jnp.where(offset <= HALF, offset + HALF, offset - HALF)
    pick = one_hot((WIN, 2 * WIN), lambda r, c: c == r + start)
    place = one_hot((2 * WIN, WIN), lambda r, c: r == c + start)
    head = lax.broadcasted_iota(jnp.int32, (WIN, 4 * HD), 1) // HD
    masks = [jnp.where(head == h, 1.0, 0.0).astype(BF16) for h in range(4)]

    for i in range(4):
        halo[2 * i].wait_recv()
        halo[2 * i + 1].wait_recv()
        win[i] = mm(pick, cat[i]).astype(BF16)
        if i == 0:
            cot_out[...] = win[0]
            dattn[...] = mm(win[0], weight_v[...], NT).astype(BF16)

    def spread(x):
        return jnp.concatenate([x * mask for mask in masks], 0)

    def lanes(x):
        return jnp.concatenate([x[h] for h in range(4)], 1)

    for g in range(4):
        cols = slice(g * 256, g * 256 + 256)
        k4, q4, v4, d4 = win[1, :, cols], win[2, :, cols], win[3, :, cols], dattn[:, cols]
        kbd, qbd, vbd, dbd = spread(k4), spread(q4), spread(v4), spread(d4)
        scores = (mm(kbd, q4, NT) * 0.125).reshape(4, WIN, WIN)
        expo = jnp.exp(scores - jnp.max(scores, axis=1, keepdims=True))
        probs = expo / jnp.sum(expo, axis=1, keepdims=True)
        low = probs.astype(BF16)
        dprob = mm(vbd, d4, NT).reshape(4, WIN, WIN)
        delta = jnp.sum(probs * dprob, axis=1, keepdims=True)
        dscore = (probs * (dprob - delta) * 0.125).astype(BF16)
        attn_out[:, cols] = mm(low.reshape(4 * WIN, WIN), vbd, TN).astype(BF16)
        qgrad = mm(dscore.reshape(4 * WIN, WIN), kbd, TN).astype(BF16)
        kgrad = mm(lanes(dscore), qbd).astype(BF16)
        vgrad = mm(lanes(low), dbd).astype(BF16)
        outs[1, :, cols] = mm(place, qgrad).astype(BF16)
        outs[2, :, cols] = mm(place, kgrad).astype(BF16)
        outs[3, :, cols] = mm(place, vgrad).astype(BF16)

    cot_basis = mm_split(basis[...], win[0], NT)
    part = mm_split(cot_basis, attn_out[...]) * GRAD_SCALE
    own = mm_exact(basis[...], error[...], NT)
    mine = one_hot((RANK, WIDTH), lambda r, c: c == r + me * RANK)
    to_tiles(left, part + mm_split(own, mine))
    for i in range(4):
        rows = slice(i * 256, i * 256 + 256)
        part = mm(attn_out[:, rows], win[0], TN) * GRAD_SCALE
        grad[i * 4 : i * 4 + 4] = part.reshape(4, 2, 32, WIDTH)
    proj[...] = mm(attn_out[...], weight_v[...]).astype(BF16)
    outs[0] = mm(place, proj[...]).astype(BF16)
    for copy in halo:
        copy.wait_send()


def combine_kernel(
    tiles, grad, outs, attn, cot, error,
    projected, qgrad, kgrad, vgrad, update, new_error, new_basis,
    scat, sums, gath, tiles_b, own_c, recv_c, send_x, recv_x, mid, recv_y, own_out, ret_prev, ret_next,
    send_sem, recv_sem, big_send, big_recv, local_sem,
):
    me = lax.axis_index("tok")
    rep = lax.axis_index("rep")
    core, y, x = lax.rem(me, 2), lax.rem(me // 2, 4), me // 8
    barrier = pltpu.get_barrier_semaphore()

    def greet_tok(k, carry):
        pl.semaphore_signal(barrier, inc=1, device_id={"tok": lax.rem(me + k, TOK)}, device_id_type=MESH)
        return carry

    def greet_rep(k, carry):
        pl.semaphore_signal(barrier, inc=1, device_id={"rep": lax.rem(rep + k, REP)}, device_id_type=MESH)
        return carry

    lax.fori_loop(1, TOK, greet_tok, 0)
    lax.fori_loop(1, REP, greet_rep, 0)
    local = [
        pltpu.make_async_copy(grad.at[:, core], own_c, local_sem.at[0]),
        pltpu.make_async_copy(outs.at[:, pl.ds(HALF, WIN)], own_out, local_sem.at[1]),
    ]
    for copy in local:
        copy.start()
    pl.semaphore_wait(barrier, TOK + REP - 2)

    def tok_send(n, phase, source, target):
        def step(k, carry):
            dev = lax.rem(me + k, TOK)
            pltpu.make_async_remote_copy(
                source(dev), target.at[k], send_sem.at[n, phase], recv_sem.at[n, phase],
                device_id={"tok": dev}, device_id_type=MESH,
            ).start()
            return carry

        lax.fori_loop(1, TOK, step, 0)

    def rep_send(n, target):
        def step(k, carry):
            pltpu.make_async_remote_copy(
                target.at[0], target.at[k], send_sem.at[n, 1], recv_sem.at[n, 1],
                device_id={"rep": lax.rem(rep + k, REP)}, device_id_type=MESH,
            ).start()
            return carry

        lax.fori_loop(1, REP, step, 0)

    def arrived(sem, ref, count):
        part = ref.at[pl.ds(1, count - 1)]
        pltpu.make_async_copy(part, part, sem).wait()

    def remote(src, dst, i, dev):
        return pltpu.make_async_remote_copy(
            src, dst, big_send.at[i], big_recv.at[i], device_id={"tok": dev}, device_id_type=MESH
        )

    def reduce_tok(n, source):
        arrived(recv_sem.at[n, 0], scat.at[n], TOK)
        total = source[me]
        for k in range(1, TOK):
            total = total + scat[n, k]
        sums[n, 0] = total
        rep_send(n, sums.at[n])

    def reduce_rep(n):
        arrived(recv_sem.at[n, 1], sums.at[n], REP)
        total = sums[n, lax.rem(rep + REP, REP)]
        for j in range(1, REP):
            total = total + sums[n, lax.rem(rep + REP - j, REP)]
        gath[n, 0] = total * (1.0 / REP)
        tok_send(n, 2, lambda dev: gath.at[n, 0], gath.at[n])

    def gathered(n):
        arrived(recv_sem.at[n, 2], gath.at[n], TOK)
        return jnp.concatenate(
            [
                jnp.concatenate([gath[n, lax.rem(me + TOK - (i * 8 + j), TOK)] for j in range(8)], 1)
                for i in range(4)
            ],
            0,
        )

    tok_send(0, 0, lambda dev: tiles.at[dev], scat.at[0])
    swap = remote(grad.at[:, 1 - core], recv_c, 0, me + 1 - 2 * core)
    swap.start()
    reduce_tok(0, tiles)

    local[0].wait()
    swap.wait_recv()
    over_x = []
    for k in range(1, 4):
        to = lax.rem(x + k, 4)
        send_x[k - 1] = (own_c[pl.ds(4 * to, 4)] + recv_c[pl.ds(4 * to, 4)]).astype(BF16)
        over_x.append(remote(send_x.at[k - 1], recv_x.at[k - 1], k, me + 8 * (to - x)))
        over_x[-1].start()

    reduce_rep(0)
    prev_dev, next_dev = lax.rem(me + TOK - 1, TOK), lax.rem(me + 1, TOK)
    back = [
        remote(outs.at[:, pl.ds(0, HALF)], ret_next, 7, prev_dev),
        remote(outs.at[:, pl.ds(HALF + WIN, HALF)], ret_prev, 8, next_dev),
    ]
    for copy in back:
        copy.start()

    left = gathered(0)
    mine = one_hot((RANK, WIDTH), lambda r, c: c == r + me * RANK)
    left_mine = mm_split(left, mine, NT)
    attn_left = mm_split(left, attn[...], NT)
    part = mm_split(attn_left, cot[...]) * GRAD_SCALE
    to_tiles(tiles_b, part + mm_exact(left_mine, error[...]))
    tok_send(1, 0, lambda dev: tiles_b.at[dev], scat.at[1])

    rows = lax.broadcasted_iota(jnp.int32, (RANK, 1), 0)
    eye = lax.broadcasted_iota(jnp.int32, (RANK, RANK), 0) == lax.broadcasted_iota(jnp.int32, (RANK, RANK), 1)
    gram = mm_exact(left, left, NT)
    inverse = jnp.where(eye, 1.0, 0.0)
    for j in range(RANK - 1):
        factor = jnp.where(rows > j, gram[:, j : j + 1], 0.0) * (1.0 / gram[j : j + 1, j : j + 1])
        gram, inverse = gram - factor * gram[j : j + 1], inverse - factor * inverse[j : j + 1]
    pivots = jnp.sum(jnp.where(eye, gram, 0.0), axis=1, keepdims=True)
    inverse = inverse * (1.0 / jnp.sqrt(pivots))
    ortho_mine = mm_exact(inverse, left_mine)

    reduce_tok(1, tiles_b)

    for copy in over_x:
        copy.wait_recv()
    mid[...] = own_c[pl.ds(4 * x, 4)] + recv_c[pl.ds(4 * x, 4)]
    for k in range(3):
        mid[...] += recv_x[k].astype(F32)
    over_y = []
    for k in range(1, 4):
        to = lax.rem(y + k, 4)
        over_y.append(remote(mid.at[to], recv_y.at[k - 1], 3 + k, me + 2 * (to - y)))
        over_y[-1].start()

    reduce_rep(1)
    for copy in over_y:
        copy.wait_recv()
    merged = mid[y] + recv_y[0] + recv_y[1] + recv_y[2] + error[...]
    new_error[...] = merged

    for copy in back:
        copy.wait_recv()
    local[1].wait()
    for i, out in enumerate((projected, qgrad, kgrad, vgrad)):
        out[0:HALF] = own_out[i, 0:HALF] + ret_prev[i]
        out[HALF:WIN] = own_out[i, HALF:WIN] + ret_next[i]

    product = gathered(1)
    basis_t = mm_exact(inverse, product)
    low_rank = mm_exact(ortho_mine, basis_t, TN)
    update[...] = low_rank
    new_error[...] = new_error[...] - low_rank
    new_basis[...] = basis_t.T

    for n in range(2):
        for phase, count in ((0, TOK), (1, REP), (2, TOK)):
            arrived(send_sem.at[n, phase], scat.at[n] if count == TOK else sums.at[n], count)
    swap.wait_send()
    for copy in over_x + over_y + back:
        copy.wait_send()


def body(
    query_rows, key_rows, value_rows, cotangent, out_weight, error_rows, window_shift, basis_seed
):
    basis = seeded_basis_t(basis_seed[0])
    error = error_rows[0]
    vmem = pl.BlockSpec(memory_space=pltpu.VMEM)
    anywhere = pl.BlockSpec(memory_space=pl.ANY)
    outs, grad, left, attn, cot = pl.pallas_call(
        attend_kernel,
        out_shape=(
            jax.ShapeDtypeStruct((4, 2 * WIN, WIDTH), BF16),
            jax.ShapeDtypeStruct((16, 2, RANK, WIDTH), F32),
            jax.ShapeDtypeStruct((TOK, 8, 128), F32),
            jax.ShapeDtypeStruct((WIN, WIDTH), BF16),
            jax.ShapeDtypeStruct((WIN, WIDTH), BF16),
        ),
        in_specs=[pl.BlockSpec(memory_space=pltpu.SMEM)] + [anywhere] * 5 + [vmem] * 2,
        out_specs=(vmem,) * 5,
        scratch_shapes=[
            pltpu.VMEM((4, 2 * WIN, WIDTH), BF16),
            pltpu.VMEM((WIDTH, WIDTH), BF16),
            pltpu.VMEM((4, WIN, WIDTH), BF16),
            pltpu.VMEM((WIN, WIDTH), BF16),
            pltpu.VMEM((WIN, WIDTH), BF16),
            pltpu.SemaphoreType.DMA((8,)),
            pltpu.SemaphoreType.DMA((8,)),
            pltpu.SemaphoreType.DMA((5,)),
        ],
        compiler_params=pltpu.CompilerParams(
            collective_id=0, has_side_effects=True, vmem_limit_bytes=48 * 2**20
        ),
        name="attend",
    )(window_shift, query_rows[0], key_rows[0], value_rows[0], cotangent[0], out_weight, basis, error)
    rows = jax.ShapeDtypeStruct((WIN, WIDTH), BF16)
    square = jax.ShapeDtypeStruct((RANK, WIDTH), F32)
    projected, qgrad, kgrad, vgrad, update, new_error, new_basis = pl.pallas_call(
        combine_kernel,
        out_shape=(rows,) * 4 + (square, square, jax.ShapeDtypeStruct((WIDTH, RANK), F32)),
        in_specs=[vmem, anywhere, anywhere, vmem, vmem, vmem],
        out_specs=(vmem,) * 7,
        scratch_shapes=[
            pltpu.VMEM((2, TOK, 8, 128), F32),
            pltpu.VMEM((2, REP, 8, 128), F32),
            pltpu.VMEM((2, TOK, 8, 128), F32),
            pltpu.VMEM((TOK, 8, 128), F32),
            pltpu.VMEM((16, RANK, WIDTH), F32),
            pltpu.VMEM((16, RANK, WIDTH), F32),
            pltpu.VMEM((3, 4, RANK, WIDTH), BF16),
            pltpu.VMEM((3, 4, RANK, WIDTH), BF16),
            pltpu.VMEM((4, RANK, WIDTH), F32),
            pltpu.VMEM((3, RANK, WIDTH), F32),
            pltpu.VMEM((4, WIN, WIDTH), BF16),
            pltpu.VMEM((4, HALF, WIDTH), BF16),
            pltpu.VMEM((4, HALF, WIDTH), BF16),
            pltpu.SemaphoreType.DMA((2, 3)),
            pltpu.SemaphoreType.DMA((2, 3)),
            pltpu.SemaphoreType.DMA((9,)),
            pltpu.SemaphoreType.DMA((9,)),
            pltpu.SemaphoreType.DMA((2,)),
        ],
        compiler_params=pltpu.CompilerParams(
            collective_id=1, has_side_effects=True, vmem_limit_bytes=48 * 2**20
        ),
        name="combine",
    )(left, grad, outs, attn, cot, error)
    return (
        projected[None],
        qgrad[None],
        kgrad[None],
        vgrad[None],
        update,
        new_error[None],
        new_basis,
    )


def solution(mesh):
    return jax.shard_map(
        body,
        mesh=mesh,
        in_specs=(
            P("rep", "tok", None),
            P("rep", "tok", None),
            P("rep", "tok", None),
            P("rep", "tok", None),
            P(),
            P("rep", "tok", None),
            P("rep"),
            P(),
        ),
        out_specs=(
            P("rep", "tok", None),
            P("rep", "tok", None),
            P("rep", "tok", None),
            P("rep", "tok", None),
            P("tok", None),
            P("rep", "tok", None),
            P(),
        ),
        check_vma=False,
    )
```

```python
import math

import jax
import jax.numpy as jnp
from jax import lax
from jax.experimental import pallas as pl
from jax.experimental.pallas import tpu as pltpu
from jax.sharding import PartitionSpec as P

H = 16
HD = 64
WIN = 128
HALF = 64
RANK = 32
WIDTH = 1024
TOK = 32
REP = 16
GROUP = 64
LONG = 8
GRAD_SCALE = 1.0 / 64.0
F32 = jnp.float32
BF16 = jnp.bfloat16
MESH = pl.DeviceIdType.MESH
HIGHEST = lax.Precision.HIGHEST
NN = (((1,), (0,)), ((), ()))
NT = (((1,), (1,)), ((), ()))
TN = (((0,), (0,)), ((), ()))


def seeded_basis_t(seed_value):
    row_index = jnp.arange(WIDTH, dtype=jnp.int32)[None, :]
    col_index = jnp.arange(RANK, dtype=jnp.int32)[:, None]
    mixed = (row_index * 7919 + col_index * 31337 + seed_value * 17 + 12345) % 65521
    mixed = (mixed * 3877 + 29) % 65521
    mixed = (mixed * 2011 + 7) % 65521
    return mixed.astype(F32) / 65521.0 - 0.5


def mm(a, b, dims=NN):
    return lax.dot_general(a, b, dims, preferred_element_type=F32)


def mm_exact(a, b, dims=NN):
    return lax.dot_general(a, b, dims, precision=HIGHEST, preferred_element_type=F32)


def mm_split(a, b, dims=NN):
    high = a.astype(BF16)
    rest = a - high.astype(F32)
    middle = rest.astype(BF16)
    low = (rest - middle.astype(F32)).astype(BF16)
    out = mm(jnp.concatenate([high, middle, low], 0), b, dims)
    return (out[2 * RANK :] + out[RANK : 2 * RANK]) + out[:RANK]


def one_hot(shape, row_to_col):
    rows = lax.broadcasted_iota(jnp.int32, shape, 0)
    cols = lax.broadcasted_iota(jnp.int32, shape, 1)
    return jnp.where(row_to_col(rows, cols), 1.0, 0.0).astype(BF16)


def halo_kernel(query, key, value, cot, cat, send_sem, recv_sem, local_sem):
    me = lax.axis_index("tok")
    next_dev, prev_dev = (me + 1) & (TOK - 1), (me + TOK - 1) & (TOK - 1)
    barrier = pltpu.get_barrier_semaphore()
    for dev in (next_dev, prev_dev):
        pl.semaphore_signal(barrier, inc=1, device_id={"tok": dev}, device_id_type=MESH)
    sources = (cot, key, query, value)
    copies = [
        pltpu.make_async_copy(src, cat.at[i, pl.ds(HALF, WIN)], local_sem.at[i])
        for i, src in enumerate(sources)
    ]
    for copy in copies:
        copy.start()
    pl.semaphore_wait(barrier, 2)
    for i, src in enumerate(sources):
        for j, (rows, place, dev) in enumerate(((0, HALF + WIN, prev_dev), (HALF, 0, next_dev))):
            copies.append(
                pltpu.make_async_remote_copy(
                    src.at[pl.ds(rows, HALF)], cat.at[i, pl.ds(place, HALF)],
                    send_sem.at[2 * i + j], recv_sem.at[2 * i + j],
                    device_id={"tok": dev}, device_id_type=MESH,
                )
            )
            copies[-1].start()
    for copy in copies:
        copy.wait()


def main_kernel(
    shift, cat, weight, basis, error_rows,
    projected, qgrad, kgrad, vgrad, update, new_error, new_basis,
    weight_v, error, win, dattn, attn, probs_s, outs, grad, recv_c, send_x, recv_x, mid, send_y, recv_y,
    ret_prev, ret_next, chunks, scat, sums, gath, whole,
    send_sem, recv_sem, big_send, big_recv, local_sem,
):
    me = lax.axis_index("tok")
    rep = lax.axis_index("rep")
    core, y_hi, x = me & 1, (me >> 1) & 3, me >> 3
    y_lo, z = rep >> 3, rep & 7
    member = (x * 2 + core) * 8 + z
    y = y_hi * 2 + y_lo
    next_dev, prev_dev = (me + 1) & (TOK - 1), (me + TOK - 1) & (TOK - 1)

    def in_group(k):
        to = (member + k) & (GROUP - 1)
        return to, {"tok": ((to >> 4) << 3) + y_hi * 2 + ((to >> 3) & 1), "rep": y_lo * 8 + (to & 7)}

    def in_y(k):
        to = (y + k) & (LONG - 1)
        return {"tok": x * 8 + (to >> 1) * 2 + core, "rep": (to & 1) * 8 + z}

    barrier = pltpu.get_barrier_semaphore()

    def greet(dev):
        pl.semaphore_signal(barrier, inc=1, device_id=dev, device_id_type=MESH)

    @pl.loop(1, GROUP)
    def _(k):
        greet(in_group(k)[1])

    @pl.loop(1, LONG)
    def _(k):
        greet(in_y(k))

    outer = core * next_dev + (1 - core) * prev_dev
    greet({"tok": outer})
    load_weight = pltpu.make_async_copy(weight, weight_v, local_sem.at[0])
    load_error = pltpu.make_async_copy(error_rows, error, local_sem.at[1])
    load_error.start()
    load_weight.start()

    def group_send(n, phase, source, target):
        @pl.loop(1, GROUP)
        def _(k):
            to, dev = in_group(k)
            pltpu.make_async_remote_copy(
                source(to), target(k), send_sem.at[n, phase], recv_sem.at[n, phase],
                device_id=dev, device_id_type=MESH,
            ).start()

    def arrived(sem, ref, count):
        part = ref.at[pl.ds(1, count - 1)]
        pltpu.make_async_copy(part, part, sem).wait()

    def remote(src, dst, i, dev):
        return pltpu.make_async_remote_copy(
            src, dst, big_send.at[i], big_recv.at[i], device_id={"tok": dev}, device_id_type=MESH
        )

    def scatter(n, field):
        for i in range(8):
            for j in range(8):
                chunks[n, i * 8 + j] = field[i * 4 : i * 4 + 4, j * 128 : j * 128 + 128]
        group_send(n, 0, lambda to: chunks.at[n, to], lambda k: scat.at[n, k])

    def reduce_group(n):
        arrived(recv_sem.at[n, 0], scat.at[n], GROUP)
        total = chunks[n, member]
        for k in range(1, GROUP):
            total = total + scat[n, k]
        sums[n, y] = total

        @pl.loop(1, LONG)
        def _(k):
            pltpu.make_async_remote_copy(
                sums.at[n, y], sums.at[n, y], send_sem.at[n, 1], recv_sem.at[n, 1],
                device_id=in_y(k), device_id_type=MESH,
            ).start()

    def reduce_y(n):
        arrived(recv_sem.at[n, 1], sums.at[n], LONG)
        total = sums[n, 0]
        for j in range(1, LONG):
            total = total + sums[n, j]
        gath[n, member] = total * (1.0 / REP)
        group_send(n, 2, lambda to: gath.at[n, member], lambda k: gath.at[n, member])

    def gathered(n):
        arrived(recv_sem.at[n, 2], gath.at[n], GROUP)
        for i in range(8):
            for j in range(8):
                whole[n, i * 4 : i * 4 + 4, j * 128 : j * 128 + 128] = gath[n, i * 8 + j]
        return whole[n]

    offset = shift[0]
    start = jnp.where(offset <= HALF, offset + HALF, offset - HALF)
    pick = one_hot((WIN, 2 * WIN), lambda r, c: c == r + start)
    place = one_hot((2 * WIN, WIN), lambda r, c: r == c + start)
    head = lax.broadcasted_iota(jnp.int32, (WIN, 4 * HD), 1) // HD
    masks = [jnp.where(head == h, 1.0, 0.0).astype(BF16) for h in range(4)]

    def spread(a):
        return jnp.concatenate([a * mask for mask in masks], 0)

    def lanes(a):
        return jnp.concatenate([a[h] for h in range(4)], 1)

    for i in range(4):
        win[i] = mm(pick, cat[i]).astype(BF16)
    for g in range(4):
        cols = slice(g * 256, g * 256 + 256)
        kbd, vbd = spread(win[1, :, cols]), spread(win[3, :, cols])
        scores = (mm(kbd, win[2, :, cols], NT) * 0.125).reshape(4, WIN, WIN)
        expo = jnp.exp(scores - jnp.max(scores, axis=1, keepdims=True))
        probs = expo / jnp.sum(expo, axis=1, keepdims=True)
        probs_s[g] = probs
        attn[:, cols] = mm(probs.astype(BF16).reshape(4 * WIN, WIN), vbd, TN).astype(BF16)

    cot = win.at[0]
    cot_basis = mm_split(basis[...], cot[...], NT)
    part = mm_split(cot_basis, attn[...]) * GRAD_SCALE
    load_error.wait()
    own = mm_exact(basis[...], error[...], NT)
    mine = one_hot((RANK, WIDTH), lambda r, c: c == r + me * RANK)
    part = part + mm_split(own, mine)
    pl.semaphore_wait(barrier, GROUP + LONG - 1)
    scatter(0, part)

    for i in range(4):
        rows = slice(i * 256, i * 256 + 256)
        part = mm(attn[:, rows], cot[...], TN) * GRAD_SCALE
        grad[i * 4 : i * 4 + 4] = part.reshape(4, 2, 32, WIDTH)
    swap = remote(grad.at[:, 1 - core], recv_c, 0, me + 1 - 2 * core)
    swap.start()

    load_weight.wait()
    dattn[...] = mm(cot[...], weight_v[...], NT).astype(BF16)

    def backward(g):
        cols = slice(g * 256, g * 256 + 256)
        k4, q4, v4, d4 = win[1, :, cols], win[2, :, cols], win[3, :, cols], dattn[:, cols]
        probs = probs_s[g]
        low = probs.astype(BF16)
        dprob = mm(spread(v4), d4, NT).reshape(4, WIN, WIN)
        delta = jnp.sum(probs * dprob, axis=1, keepdims=True)
        dscore = (probs * (dprob - delta) * 0.125).astype(BF16)
        results = (
            mm(dscore.reshape(4 * WIN, WIN), spread(k4), TN),
            mm(lanes(dscore), spread(q4)),
            mm(lanes(low), spread(d4)),
        )
        for i, result in enumerate(results):
            outs[1 + i, :, cols] = mm(place, result.astype(BF16)).astype(BF16)

    backward(0)
    backward(1)
    reduce_group(0)

    def ring(index, count_dev, send, recv, first, part, half):
        up, down, far = (index + 1) & 3, (index + 3) & 3, (index + 2) & 3
        to_up, to_down = count_dev(up), count_dev(down)
        send[0, 0] = part(far, 0).astype(BF16)
        send[1, 0] = part(far, 1).astype(BF16)
        send[0, 1] = part(up, 1).astype(BF16)
        send[1, 1] = part(down, 0).astype(BF16)
        copies = {
            (d, i): remote(send.at[d, i], recv.at[d, i], first + 3 * d + i, dev)
            for d, dev in enumerate((to_up, to_down))
            for i in range(3)
        }
        for i in range(2):
            for d in range(2):
                copies[d, i].start()

        def forward():
            for d, (to, rows) in enumerate(((up, 0), (down, 1))):
                copies[d, 0].wait_recv()
                send[d, 2] = (part(to, rows) + recv[d, 0].astype(F32)).astype(BF16)
                copies[d, 2].start()

        def total(rows):
            one, two = ((0, 2), (1, 1)) if rows == 0 else ((1, 2), (0, 1))
            return part(index, rows) + recv[one].astype(F32) + recv[two].astype(F32)

        def wait_total():
            for d in range(2):
                copies[d, 1].wait_recv()
                copies[d, 2].wait_recv()

        return copies, forward, wait_total, total

    def part_x(to, rows):
        blocks = pl.ds(4 * to + 2 * rows, 2)
        return grad[blocks, core] + recv_c[blocks]

    def part_y(to, rows):
        return mid[to, rows * 16 : rows * 16 + 16]

    swap.wait_recv()
    copies_x, forward_x, wait_x, total_x = ring(
        x, lambda to: to * 8 + y_hi * 2 + core, send_x, recv_x, 1, part_x, 2
    )

    backward(2)
    backward(3)
    outs[0] = mm(place, mm(attn[...], weight_v[...]).astype(BF16)).astype(BF16)
    reduce_y(0)
    back = [
        remote(outs.at[:, pl.ds(0, HALF)], ret_next, 13, prev_dev),
        remote(outs.at[:, pl.ds(HALF + WIN, HALF)], ret_prev, 14, next_dev),
    ]
    for copy in back:
        copy.start()
    forward_x()

    left = gathered(0)
    left_mine = mm_split(left, mine, NT)
    attn_left = mm_split(left, attn[...], NT)
    part = mm_split(attn_left, cot[...]) * GRAD_SCALE
    scatter(1, part + mm_exact(left_mine, error[...]))

    rows = lax.broadcasted_iota(jnp.int32, (RANK, 1), 0)
    eye = lax.broadcasted_iota(jnp.int32, (RANK, RANK), 0) == lax.broadcasted_iota(jnp.int32, (RANK, RANK), 1)
    gram = mm_exact(left, left, NT)
    inverse = jnp.where(eye, 1.0, 0.0)
    for j in range(RANK - 1):
        factor = jnp.where(rows > j, gram[:, j : j + 1], 0.0) * (1.0 / gram[j : j + 1, j : j + 1])
        gram, inverse = gram - factor * gram[j : j + 1], inverse - factor * inverse[j : j + 1]
    pivots = jnp.sum(jnp.where(eye, gram, 0.0), axis=1, keepdims=True)
    inverse = inverse * (1.0 / jnp.sqrt(pivots))
    ortho_mine = mm_exact(inverse, left_mine)

    reduce_group(1)
    wait_x()
    for rows in range(2):
        mid[2 * rows : 2 * rows + 2] = total_x(rows)
    copies_y, forward_y, wait_y, total_y = ring(
        y_hi, lambda to: x * 8 + to * 2 + core, send_y, recv_y, 7, part_y, 16
    )
    reduce_y(1)
    forward_y()

    for copy in back:
        copy.wait_recv()
    for i, out in enumerate((projected, qgrad, kgrad, vgrad)):
        out[0:HALF] = outs[i, HALF:WIN] + ret_prev[i]
        out[HALF:WIN] = outs[i, WIN : WIN + HALF] + ret_next[i]

    product = gathered(1)
    basis_t = mm_exact(inverse, product)
    low_rank = mm_exact(ortho_mine, basis_t, TN)
    update[...] = low_rank
    new_basis[...] = basis_t
    wait_y()
    for rows in range(2):
        at = slice(rows * 16, rows * 16 + 16)
        new_error[at] = total_y(rows) + error[at] - low_rank[at]

    for n in range(2):
        for phase, ref, count in ((0, scat, GROUP), (1, sums, LONG), (2, gath, GROUP)):
            arrived(send_sem.at[n, phase], ref.at[n], count)
    swap.wait_send()
    for copy in [*copies_x.values(), *copies_y.values(), *back]:
        copy.wait_send()


def place_kernel(*refs):
    count = len(refs) // 2
    sems = refs[-1]
    copies = [pltpu.make_async_copy(refs[i], refs[count + i], sems.at[i]) for i in range(count)]
    for copy in copies:
        copy.start()
    for copy in copies:
        copy.wait()


def stay(array):
    return pltpu.with_memory_space_constraint(array, pltpu.HBM)


def body(
    query_rows, key_rows, value_rows, cotangent, out_weight, error_rows, window_shift, basis_seed
):
    basis = seeded_basis_t(basis_seed[0])
    error = error_rows[0]
    vmem = pl.BlockSpec(memory_space=pltpu.VMEM)
    hbm = pl.BlockSpec(memory_space=pltpu.HBM)
    cat = pl.pallas_call(
        halo_kernel,
        out_shape=jax.ShapeDtypeStruct((4, 2 * WIN, WIDTH), BF16),
        in_specs=[hbm] * 4,
        out_specs=vmem,
        scratch_shapes=[
            pltpu.SemaphoreType.DMA((8,)),
            pltpu.SemaphoreType.DMA((8,)),
            pltpu.SemaphoreType.DMA((4,)),
        ],
        compiler_params=pltpu.CompilerParams(collective_id=0, has_side_effects=True, vmem_limit_bytes=8 * 2**20),
        name="halo",
    )(*(stay(rows[0]) for rows in (query_rows, key_rows, value_rows, cotangent)))
    rows = jax.ShapeDtypeStruct((WIN, WIDTH), BF16)
    square = jax.ShapeDtypeStruct((RANK, WIDTH), F32)
    results = (rows,) * 4 + (square,) * 3
    parts = pl.pallas_call(
        main_kernel,
        out_shape=results,
        in_specs=[pl.BlockSpec(memory_space=pltpu.SMEM), vmem, hbm, vmem, hbm],
        out_specs=(vmem,) * 7,
        scratch_shapes=[
            pltpu.VMEM((WIDTH, WIDTH), BF16),
            pltpu.VMEM((RANK, WIDTH), F32),
            pltpu.VMEM((4, WIN, WIDTH), BF16),
            pltpu.VMEM((WIN, WIDTH), BF16),
            pltpu.VMEM((WIN, WIDTH), BF16),
            pltpu.VMEM((4, 4, WIN, WIN), F32),
            pltpu.VMEM((4, 2 * WIN, WIDTH), BF16),
            pltpu.VMEM((16, 2, RANK, WIDTH), F32),
            pltpu.VMEM((16, RANK, WIDTH), F32),
            pltpu.VMEM((2, 3, 2, RANK, WIDTH), BF16),
            pltpu.VMEM((2, 3, 2, RANK, WIDTH), BF16),
            pltpu.VMEM((4, RANK, WIDTH), F32),
            pltpu.VMEM((2, 3, 16, WIDTH), BF16),
            pltpu.VMEM((2, 3, 16, WIDTH), BF16),
            pltpu.VMEM((4, HALF, WIDTH), BF16),
            pltpu.VMEM((4, HALF, WIDTH), BF16),
            pltpu.VMEM((2, GROUP, 4, 128), F32),
            pltpu.VMEM((2, GROUP, 4, 128), F32),
            pltpu.VMEM((2, LONG, 4, 128), F32),
            pltpu.VMEM((2, GROUP, 4, 128), F32),
            pltpu.VMEM((2, RANK, WIDTH), F32),
            pltpu.SemaphoreType.DMA((2, 3)),
            pltpu.SemaphoreType.DMA((2, 3)),
            pltpu.SemaphoreType.DMA((15,)),
            pltpu.SemaphoreType.DMA((15,)),
            pltpu.SemaphoreType.DMA((2,)),
        ],
        compiler_params=pltpu.CompilerParams(
            collective_id=1, has_side_effects=True, vmem_limit_bytes=32 * 2**20
        ),
        name="main",
    )(window_shift, cat, stay(out_weight), basis, stay(error))
    projected, qgrad, kgrad, vgrad, update, new_error, new_basis = pl.pallas_call(
        place_kernel,
        out_shape=results,
        in_specs=[vmem] * 7,
        out_specs=(hbm,) * 7,
        scratch_shapes=[pltpu.SemaphoreType.DMA((7,))],
        compiler_params=pltpu.CompilerParams(vmem_limit_bytes=8 * 2**20),
        name="place",
    )(*parts)
    return (
        projected[None],
        qgrad[None],
        kgrad[None],
        vgrad[None],
        update,
        new_error[None],
        new_basis.T,
    )


def solution(mesh):
    return jax.shard_map(
        body,
        mesh=mesh,
        in_specs=(
            P("rep", "tok", None),
            P("rep", "tok", None),
            P("rep", "tok", None),
            P("rep", "tok", None),
            P(),
            P("rep", "tok", None),
            P("rep"),
            P(),
        ),
        out_specs=(
            P("rep", "tok", None),
            P("rep", "tok", None),
            P("rep", "tok", None),
            P("rep", "tok", None),
            P("tok", None),
            P("rep", "tok", None),
            P(),
        ),
        check_vma=False,
    )
```

```python
import math

import jax
import jax.numpy as jnp
from jax import lax
from jax.experimental import pallas as pl
from jax.experimental.pallas import tpu as pltpu
from jax.sharding import PartitionSpec as P

H = 16
HD = 64
WIN = 128
HALF = 64
RANK = 32
WIDTH = 1024
TOK = 32
REP = 16
LINE = 8
PRIME = 65521
GRAD_SCALE = 1.0 / 64.0
F32 = jnp.float32
BF16 = jnp.bfloat16
MESH = pl.DeviceIdType.MESH
HIGHEST = lax.Precision.HIGHEST
NN = (((1,), (0,)), ((), ()))
NT = (((1,), (1,)), ((), ()))
TN = (((0,), (0,)), ((), ()))


def mod_prime(a):
    rest = a - (a.astype(F32) * (1.0 / PRIME)).astype(jnp.int32) * PRIME
    rest = jnp.where(rest < 0, rest + PRIME, rest)
    return jnp.where(rest >= PRIME, rest - PRIME, rest)


def seeded_basis_t(seed_value):
    row_index = lax.broadcasted_iota(jnp.int32, (RANK, WIDTH), 1)
    col_index = lax.broadcasted_iota(jnp.int32, (RANK, WIDTH), 0)
    mixed = mod_prime(row_index * 7919 + col_index * 31337 + (seed_value * 17 + 12345))
    mixed = mod_prime(mixed * 3877 + 29)
    mixed = mod_prime(mixed * 2011 + 7)
    return mixed.astype(F32) / 65521.0 - 0.5


def mm(a, b, dims=NN):
    return lax.dot_general(a, b, dims, preferred_element_type=F32)


def mm_exact(a, b, dims=NN):
    return lax.dot_general(a, b, dims, precision=HIGHEST, preferred_element_type=F32)


def mm_split(a, b, dims=NN):
    high = a.astype(BF16)
    rest = a - high.astype(F32)
    middle = rest.astype(BF16)
    low = (rest - middle.astype(F32)).astype(BF16)
    out = mm(jnp.concatenate([high, middle, low], 0), b, dims)
    return (out[2 * RANK :] + out[RANK : 2 * RANK]) + out[:RANK]


def one_hot(shape, row_to_col):
    rows = lax.broadcasted_iota(jnp.int32, shape, 0)
    cols = lax.broadcasted_iota(jnp.int32, shape, 1)
    return jnp.where(row_to_col(rows, cols), 1.0, 0.0).astype(BF16)


def halo_kernel(
    seed, query, key, value, cot, error,
    cat, cot_basis, basis, error_left,
    cot_v, error_v, send_sem, recv_sem, local_sem,
):
    me = lax.axis_index("tok")
    next_dev, prev_dev = (me + 1) & (TOK - 1), (me + TOK - 1) & (TOK - 1)
    barrier = pltpu.get_barrier_semaphore()
    for dev in (next_dev, prev_dev):
        pl.semaphore_signal(barrier, inc=1, device_id={"tok": dev}, device_id_type=MESH)
    load_cot = pltpu.make_async_copy(cot, cot_v, local_sem.at[3])
    load_error = pltpu.make_async_copy(error, error_v, local_sem.at[4])
    load_cot.start()
    load_error.start()
    sources = (key, query, value)
    copies = [
        pltpu.make_async_copy(src, cat.at[i, pl.ds(HALF, WIN)], local_sem.at[i])
        for i, src in enumerate(sources)
    ]
    for copy in copies:
        copy.start()
    pl.semaphore_wait(barrier, 2)

    def remote(src, dst, i, dev):
        copies.append(
            pltpu.make_async_remote_copy(
                src, dst, send_sem.at[i], recv_sem.at[i], device_id={"tok": dev}, device_id_type=MESH
            )
        )
        copies[-1].start()

    for i, src in enumerate(sources):
        remote(src.at[pl.ds(0, HALF)], cat.at[i, pl.ds(HALF + WIN, HALF)], 2 * i, prev_dev)
        remote(src.at[pl.ds(HALF, HALF)], cat.at[i, pl.ds(0, HALF)], 2 * i + 1, next_dev)

    basis[...] = seeded_basis_t(seed[0])
    load_cot.wait()
    cot_basis[1] = mm_split(basis[...], cot_v[...], NT)
    remote(cot_basis.at[1], cot_basis.at[2], 6, prev_dev)
    remote(cot_basis.at[1], cot_basis.at[0], 7, next_dev)
    load_error.wait()
    own = mm_exact(basis[...], error_v[...], NT)
    mine = one_hot((RANK, WIDTH), lambda r, c: c == r + me * RANK)
    error_left[...] = mm_split(own, mine)
    for copy in copies:
        copy.wait()


def main_kernel(
    shift, cat, cot_basis, basis, error_left, weight, cot_rows, error_rows,
    projected, qgrad, kgrad, vgrad, update, new_error, new_basis,
    weight_v, error, cot_cat, win, dattn, attn, probs_s, outs, grad, grad_low, recv_c, send_x, recv_x, mid, send_y, recv_y,
    ret_prev, ret_next, chunks, scat, sums, gath,
    send_sem, recv_sem, big_send, big_recv, local_sem,
):
    me = lax.axis_index("tok")
    rep = lax.axis_index("rep")
    core, y_hi, x = me & 1, (me >> 1) & 3, me >> 3
    y_lo, z = rep >> 3, rep & 7
    pair = x * 2 + core
    y = y_hi * 2 + y_lo
    next_dev, prev_dev = (me + 1) & (TOK - 1), (me + TOK - 1) & (TOK - 1)

    def others(index):
        return [(index + k) & (LINE - 1) for k in (4, 3, 5, 2, 6, 1, 7)]

    steps = ((2, 0), (2, 1), (1, 0), (3, 0), (1, 1), (3, 1), (0, 1))
    along_x = [{"tok": ((x + i) & 3) * 8 + y_hi * 2 + (core ^ j)} for i, j in steps]
    along_y = [{"tok": x * 8 + (to >> 1) * 2 + core, "rep": (to & 1) * 8 + z} for to in others(y)]
    along_z = [(to, {"rep": y_lo * 8 + to}) for to in others(z)]
    barrier = pltpu.get_barrier_semaphore()

    def greet(dev):
        pl.semaphore_signal(barrier, inc=1, device_id=dev, device_id_type=MESH)

    for dev in [dev for _, dev in along_z] + along_y + along_x:
        greet(dev)
    outer = core * next_dev + (1 - core) * prev_dev
    greet({"tok": outer})
    load_weight = pltpu.make_async_copy(weight, weight_v, local_sem.at[0])
    load_error = pltpu.make_async_copy(error_rows, error, local_sem.at[1])
    load_cot = pltpu.make_async_copy(cot_rows, cot_cat.at[pl.ds(HALF, WIN)], local_sem.at[2])
    load_weight.start()
    load_cot.start()
    load_error.start()

    def small(src, dst, sems, dev):
        send, recv = send_sem.at[sems], recv_sem.at[sems]
        pltpu.make_async_remote_copy(src, dst, send, recv, device_id=dev, device_id_type=MESH).start()

    def arrived(sem, ref):
        part = ref.at[pl.ds(1, LINE - 1)]
        pltpu.make_async_copy(part, part, sem).wait()

    def remote(src, dst, i, dev):
        return pltpu.make_async_remote_copy(
            src, dst, big_send.at[i], big_recv.at[i], device_id={"tok": dev}, device_id_type=MESH
        )

    def scatter(n, field):
        for i in range(LINE):
            chunks[n, i] = field[:, i * 128 : i * 128 + 128]
        for k, (to, dev) in enumerate(along_z):
            small(chunks.at[n, to], scat.at[n, 1 + k], 4 * n, dev)

    def line_send(n, line, total):
        index, devs = ((pair, along_x), (y, along_y))[line]
        sums[n, line, index] = total
        for dev in devs:
            small(sums.at[n, line, index], sums.at[n, line, index], 4 * n + 1 + line, dev)

    def line_sum(n, line):
        arrived(recv_sem.at[4 * n + 1 + line], sums.at[n, line])
        total = sums[n, line, 0]
        for j in range(1, LINE):
            total = total + sums[n, line, j]
        return total

    def sum_group(n):
        arrived(recv_sem.at[4 * n], scat.at[n])
        total = chunks[n, z]
        for k in range(1, LINE):
            total = total + scat[n, k]
        line_send(n, 0, total)

    def sum_first(n):
        line_send(n, 1, line_sum(n, 0))

    def sum_second(n):
        gath[n, z] = line_sum(n, 1) * (1.0 / REP)
        for _, dev in along_z:
            small(gath.at[n, z], gath.at[n, z], 4 * n + 3, dev)

    def gathered(n):
        arrived(recv_sem.at[4 * n + 3], gath.at[n])
        return jnp.concatenate([gath[n, i] for i in range(LINE)], 1)

    def sent(n):
        for i, ref in enumerate((scat.at[n], sums.at[n, 0], sums.at[n, 1], gath.at[n])):
            arrived(send_sem.at[4 * n + i], ref)

    offset = shift[0]
    start = jnp.where(offset <= HALF, offset + HALF, offset - HALF)
    pick = one_hot((WIN, 2 * WIN), lambda r, c: c == r + start)
    place = one_hot((2 * WIN, WIN), lambda r, c: r == c + start)
    head = lax.broadcasted_iota(jnp.int32, (WIN, 4 * HD), 1) // HD
    masks = [jnp.where(head == h, 1.0, 0.0).astype(BF16) for h in range(4)]

    def spread(a):
        return jnp.concatenate([a * mask for mask in masks], 0)

    def lanes(a):
        return jnp.concatenate([a[h] for h in range(4)], 1)

    for i in range(3):
        win[1 + i] = mm(pick, cat[i]).astype(BF16)
    for g in range(4):
        cols = slice(g * 256, g * 256 + 256)
        kbd, vbd = spread(win[1, :, cols]), spread(win[3, :, cols])
        scores = (mm(kbd, win[2, :, cols], NT) * 0.125).reshape(4, WIN, WIN)
        expo = jnp.exp(scores - jnp.max(scores, axis=1, keepdims=True))
        probs = expo / jnp.sum(expo, axis=1, keepdims=True)
        probs_s[g] = probs
        attn[:, cols] = mm(probs.astype(BF16).reshape(4 * WIN, WIN), vbd, TN).astype(BF16)

    cot_cols = jnp.concatenate([cot_basis[i] for i in range(3)], 1)
    pick_cols = one_hot((3 * WIN, WIN), lambda r, c: r == c + start + HALF)
    part = mm_split(mm_split(cot_cols, pick_cols), attn[...]) * GRAD_SCALE + error_left[...]
    pl.semaphore_wait(barrier, 3 * (LINE - 1) + 1)
    scatter(0, part)
    cot_halo = [
        remote(cot_rows.at[pl.ds(0, HALF)], cot_cat.at[pl.ds(HALF + WIN, HALF)], 20, prev_dev),
        remote(cot_rows.at[pl.ds(HALF, HALF)], cot_cat.at[pl.ds(0, HALF)], 21, next_dev),
    ]
    for copy in cot_halo:
        copy.start()

    def send_back(i, arrays, cols):
        copies = [
            remote(outs.at[arrays, pl.ds(0, HALF), cols], ret_next.at[arrays, :, cols], i, prev_dev),
            remote(outs.at[arrays, pl.ds(HALF + WIN, HALF), cols], ret_prev.at[arrays, :, cols], i + 1, next_dev),
        ]
        for copy in copies:
            copy.start()
        return copies

    load_weight.wait()
    outs[0] = mm(place, mm(attn[...], weight_v[...]).astype(BF16)).astype(BF16)
    load_cot.wait()
    sum_group(0)
    for copy in cot_halo:
        copy.wait_recv()
    back = send_back(13, pl.ds(0, 1), pl.ds(0, WIDTH))
    cot = win.at[0]
    cot[...] = mm(pick, cot_cat[...]).astype(BF16)

    swaps = []
    for i, step in enumerate((2, 1, 3, 0)):
        to = (x + step) & 3
        cols = pl.ds(pl.multiple_of(to * 256, 256), 256)
        part = (mm(attn[:, cols], cot[...], TN) * GRAD_SCALE).reshape(4, 2, 32, WIDTH)
        blocks = pl.ds(4 * to, 4)
        grad[blocks] = jnp.where(core == 0, part[:, 0], part[:, 1])
        grad_low[blocks] = jnp.where(core == 0, part[:, 1], part[:, 0]).astype(BF16)
        swaps.append(remote(grad_low.at[blocks], recv_c.at[blocks], (0, 15, 16, 17)[i], me + 1 - 2 * core))
        swaps[-1].start()

    dattn[...] = mm(cot[...], weight_v[...], NT).astype(BF16)

    def backward(g):
        cols = slice(g * 256, g * 256 + 256)
        k4, q4, v4, d4 = win[1, :, cols], win[2, :, cols], win[3, :, cols], dattn[:, cols]
        probs = probs_s[g]
        low = probs.astype(BF16)
        dprob = mm(spread(v4), d4, NT).reshape(4, WIN, WIN)
        delta = jnp.sum(probs * dprob, axis=1, keepdims=True)
        dscore = (probs * (dprob - delta) * 0.125).astype(BF16)
        results = (
            mm(dscore.reshape(4 * WIN, WIN), spread(k4), TN),
            mm(lanes(dscore), spread(q4)),
            mm(lanes(low), spread(d4)),
        )
        for i, result in enumerate(results):
            outs[1 + i, :, cols] = mm(place, result.astype(BF16)).astype(BF16)

    def ring(index, count_dev, send, recv, first, part, ready):
        up, down, far = (index + 1) & 3, (index + 3) & 3, (index + 2) & 3
        to_up, to_down = count_dev(up), count_dev(down)
        copies = {
            (d, i): remote(send.at[d, i], recv.at[d, i], first + 3 * d + i, dev)
            for d, dev in enumerate((to_up, to_down))
            for i in range(3)
        }
        ready(0)
        for d in range(2):
            send[d, 0] = part(far, d).astype(BF16)
            copies[d, 0].start()

        def pure():
            for d, to in enumerate((up, down)):
                ready(1 + d)
                send[d, 1] = part(to, 1 - d).astype(BF16)
                copies[d, 1].start()

        def forward():
            for d, (to, rows) in enumerate(((up, 0), (down, 1))):
                copies[d, 0].wait_recv()
                send[d, 2] = (part(to, rows) + recv[d, 0].astype(F32)).astype(BF16)
                copies[d, 2].start()

        def total(rows):
            one, two = ((0, 2), (1, 1)) if rows == 0 else ((1, 2), (0, 1))
            return part(index, rows) + recv[one].astype(F32) + recv[two].astype(F32)

        def wait_total():
            ready(3)
            for d in range(2):
                copies[d, 1].wait_recv()
                copies[d, 2].wait_recv()

        return copies, pure, forward, wait_total, total

    def part_x(to, rows):
        blocks = pl.ds(4 * to + 2 * rows, 2)
        return grad[blocks] + recv_c[blocks].astype(F32)

    def part_y(to, rows):
        return mid[to, rows * 16 : rows * 16 + 16]

    backward(0)
    sum_first(0)
    copies_x, pure_x, forward_x, wait_x, total_x = ring(
        x, lambda to: to * 8 + y_hi * 2 + core, send_x, recv_x, 1, part_x, lambda i: swaps[i].wait_recv()
    )
    pure_x()
    backward(1)
    backward(2)
    backward(3)
    sum_second(0)
    back += send_back(18, pl.ds(1, 3), pl.ds(0, WIDTH))
    forward_x()

    load_error.wait()
    left = gathered(0)
    mine = one_hot((RANK, WIDTH), lambda r, c: c == r + me * RANK)
    left_mine = mm_split(left, mine, NT)
    attn_left = mm_split(left, attn[...], NT)
    part = mm_split(attn_left, cot[...]) * GRAD_SCALE
    scatter(1, part + mm_exact(left_mine, error[...]))

    wait_x()
    for rows in range(2):
        mid[2 * rows : 2 * rows + 2] = total_x(rows)
    copies_y, pure_y, forward_y, wait_y, total_y = ring(
        y_hi, lambda to: x * 8 + to * 2 + core, send_y, recv_y, 7, part_y, lambda i: None
    )
    pure_y()

    rows = lax.broadcasted_iota(jnp.int32, (RANK, 1), 0)
    eye = lax.broadcasted_iota(jnp.int32, (RANK, RANK), 0) == lax.broadcasted_iota(jnp.int32, (RANK, RANK), 1)
    gram = mm_exact(left, left, NT)
    inverse = jnp.where(eye, 1.0, 0.0)
    for j in range(RANK - 1):
        factor = jnp.where(rows > j, gram[:, j : j + 1], 0.0) * (1.0 / gram[j : j + 1, j : j + 1])
        gram, inverse = gram - factor * gram[j : j + 1], inverse - factor * inverse[j : j + 1]
    pivots = jnp.sum(jnp.where(eye, gram, 0.0), axis=1, keepdims=True)
    inverse = inverse * (1.0 / jnp.sqrt(pivots))
    ortho_mine = mm_exact(inverse, left_mine)

    sum_group(1)
    forward_y()
    sum_first(1)
    sum_second(1)

    for copy in back:
        copy.wait_recv()
    for i, out in enumerate((projected, qgrad, kgrad, vgrad)):
        out[0:HALF] = outs[i, HALF:WIN] + ret_prev[i]
        out[HALF:WIN] = outs[i, WIN : WIN + HALF] + ret_next[i]

    product = gathered(1)
    basis_t = mm_exact(inverse, product)
    low_rank = mm_exact(ortho_mine, basis_t, TN)
    update[...] = low_rank
    new_basis[...] = basis_t
    wait_y()
    for rows in range(2):
        at = slice(rows * 16, rows * 16 + 16)
        new_error[at] = total_y(rows) + error[at] - low_rank[at]

    for n in range(2):
        sent(n)
    for copy in [*swaps, *copies_x.values(), *copies_y.values(), *back, *cot_halo]:
        copy.wait_send()


def place_kernel(*refs):
    count = len(refs) // 2
    sems = refs[-1]
    copies = [pltpu.make_async_copy(refs[i], refs[count + i], sems.at[i]) for i in range(count)]
    for copy in copies:
        copy.start()
    for copy in copies:
        copy.wait()


def stay(array):
    return pltpu.with_memory_space_constraint(array, pltpu.HBM)


def body(
    query_rows, key_rows, value_rows, cotangent, out_weight, error_rows, window_shift, basis_seed
):
    error = stay(error_rows[0])
    cot_rows = stay(cotangent[0])
    smem = pl.BlockSpec(memory_space=pltpu.SMEM)
    vmem = pl.BlockSpec(memory_space=pltpu.VMEM)
    hbm = pl.BlockSpec(memory_space=pltpu.HBM)
    square = jax.ShapeDtypeStruct((RANK, WIDTH), F32)
    cat, cot_basis, basis, error_left = pl.pallas_call(
        halo_kernel,
        out_shape=(
            jax.ShapeDtypeStruct((3, 2 * WIN, WIDTH), BF16),
            jax.ShapeDtypeStruct((3, RANK, WIN), F32),
            square,
            square,
        ),
        in_specs=[smem] + [hbm] * 5,
        out_specs=(vmem,) * 4,
        scratch_shapes=[
            pltpu.VMEM((WIN, WIDTH), BF16),
            pltpu.VMEM((RANK, WIDTH), F32),
            pltpu.SemaphoreType.DMA((8,)),
            pltpu.SemaphoreType.DMA((8,)),
            pltpu.SemaphoreType.DMA((5,)),
        ],
        compiler_params=pltpu.CompilerParams(collective_id=0, has_side_effects=True, vmem_limit_bytes=8 * 2**20),
        name="halo",
    )(basis_seed, *(stay(rows[0]) for rows in (query_rows, key_rows, value_rows)), cot_rows, error)
    rows = jax.ShapeDtypeStruct((WIN, WIDTH), BF16)
    results = (rows,) * 4 + (square,) * 3
    parts = pl.pallas_call(
        main_kernel,
        out_shape=results,
        in_specs=[smem] + [vmem] * 4 + [hbm] * 3,
        out_specs=(vmem,) * 7,
        scratch_shapes=[
            pltpu.VMEM((WIDTH, WIDTH), BF16),
            pltpu.VMEM((RANK, WIDTH), F32),
            pltpu.VMEM((2 * WIN, WIDTH), BF16),
            pltpu.VMEM((4, WIN, WIDTH), BF16),
            pltpu.VMEM((WIN, WIDTH), BF16),
            pltpu.VMEM((WIN, WIDTH), BF16),
            pltpu.VMEM((4, 4, WIN, WIN), F32),
            pltpu.VMEM((4, 2 * WIN, WIDTH), BF16),
            pltpu.VMEM((16, RANK, WIDTH), F32),
            pltpu.VMEM((16, RANK, WIDTH), BF16),
            pltpu.VMEM((16, RANK, WIDTH), BF16),
            pltpu.VMEM((2, 3, 2, RANK, WIDTH), BF16),
            pltpu.VMEM((2, 3, 2, RANK, WIDTH), BF16),
            pltpu.VMEM((4, RANK, WIDTH), F32),
            pltpu.VMEM((2, 3, 16, WIDTH), BF16),
            pltpu.VMEM((2, 3, 16, WIDTH), BF16),
            pltpu.VMEM((4, HALF, WIDTH), BF16),
            pltpu.VMEM((4, HALF, WIDTH), BF16),
            pltpu.VMEM((2, LINE, RANK, 128), F32),
            pltpu.VMEM((2, LINE, RANK, 128), F32),
            pltpu.VMEM((2, 2, LINE, RANK, 128), F32),
            pltpu.VMEM((2, LINE, RANK, 128), F32),
            pltpu.SemaphoreType.DMA((8,)),
            pltpu.SemaphoreType.DMA((8,)),
            pltpu.SemaphoreType.DMA((22,)),
            pltpu.SemaphoreType.DMA((22,)),
            pltpu.SemaphoreType.DMA((3,)),
        ],
        compiler_params=pltpu.CompilerParams(
            collective_id=1, has_side_effects=True, vmem_limit_bytes=32 * 2**20
        ),
        name="main",
    )(window_shift, cat, cot_basis, basis, error_left, stay(out_weight), cot_rows, error)
    projected, qgrad, kgrad, vgrad, update, new_error, new_basis = pl.pallas_call(
        place_kernel,
        out_shape=results,
        in_specs=[vmem] * 7,
        out_specs=(hbm,) * 7,
        scratch_shapes=[pltpu.SemaphoreType.DMA((7,))],
        compiler_params=pltpu.CompilerParams(vmem_limit_bytes=8 * 2**20),
        name="place",
    )(*parts)
    return (
        projected[None],
        qgrad[None],
        kgrad[None],
        vgrad[None],
        update,
        new_error[None],
        new_basis.T,
    )


def solution(mesh):
    return jax.shard_map(
        body,
        mesh=mesh,
        in_specs=(
            P("rep", "tok", None),
            P("rep", "tok", None),
            P("rep", "tok", None),
            P("rep", "tok", None),
            P(),
            P("rep", "tok", None),
            P("rep"),
            P(),
        ),
        out_specs=(
            P("rep", "tok", None),
            P("rep", "tok", None),
            P("rep", "tok", None),
            P("rep", "tok", None),
            P("tok", None),
            P("rep", "tok", None),
            P(),
        ),
        check_vma=False,
    )
```

```python
import math

import jax
import jax.numpy as jnp
from jax import lax
from jax.experimental import pallas as pl
from jax.experimental.pallas import tpu as pltpu
from jax.sharding import PartitionSpec as P

H = 16
HD = 64
WIN = 128
HALF = 64
RANK = 32
WIDTH = 1024
TOK = 32
REP = 16
LINE = 8
PRIME = 65521
GRAD_SCALE = 1.0 / 64.0
F32 = jnp.float32
BF16 = jnp.bfloat16
MESH = pl.DeviceIdType.MESH
HIGHEST = lax.Precision.HIGHEST
NN = (((1,), (0,)), ((), ()))
NT = (((1,), (1,)), ((), ()))
TN = (((0,), (0,)), ((), ()))


def mod_prime(a):
    rest = a - (a.astype(F32) * (1.0 / PRIME)).astype(jnp.int32) * PRIME
    rest = jnp.where(rest < 0, rest + PRIME, rest)
    return jnp.where(rest >= PRIME, rest - PRIME, rest)


def seeded_basis_t(seed_value):
    row_index = lax.broadcasted_iota(jnp.int32, (RANK, WIDTH), 1)
    col_index = lax.broadcasted_iota(jnp.int32, (RANK, WIDTH), 0)
    mixed = mod_prime(row_index * 7919 + col_index * 31337 + (seed_value * 17 + 12345))
    mixed = mod_prime(mixed * 3877 + 29)
    mixed = mod_prime(mixed * 2011 + 7)
    return mixed.astype(F32) / 65521.0 - 0.5


def mm(a, b, dims=NN):
    return lax.dot_general(a, b, dims, preferred_element_type=F32)


def mm_exact(a, b, dims=NN):
    return lax.dot_general(a, b, dims, precision=HIGHEST, preferred_element_type=F32)


def mm_split(a, b, dims=NN):
    high = a.astype(BF16)
    rest = a - high.astype(F32)
    middle = rest.astype(BF16)
    low = (rest - middle.astype(F32)).astype(BF16)
    out = mm(jnp.concatenate([high, middle, low], 0), b, dims)
    return (out[2 * RANK :] + out[RANK : 2 * RANK]) + out[:RANK]


def one_hot(shape, row_to_col):
    rows = lax.broadcasted_iota(jnp.int32, shape, 0)
    cols = lax.broadcasted_iota(jnp.int32, shape, 1)
    return jnp.where(row_to_col(rows, cols), 1.0, 0.0).astype(BF16)


def main_kernel(
    seed, shift, query, key, value, cot_rows, weight, error_rows,
    projected, qgrad, kgrad, vgrad, update, new_error, new_basis,
    cat, cot_basis, basis, error_left, weight_v, error, cot_cat, win, dattn, attn, probs_s, outs, grad, grad_low, recv_c, send_x, recv_x, mid, send_y, recv_y,
    ret_prev, ret_next, chunks, scat, sums, gath,
    send_sem, recv_sem, big_send, big_recv, halo_send, halo_recv, local_sem,
):
    me = lax.axis_index("tok")
    rep = lax.axis_index("rep")
    core, y_hi, x = me & 1, (me >> 1) & 3, me >> 3
    y_lo, z = rep >> 3, rep & 7
    pair = x * 2 + core
    y = y_hi * 2 + y_lo
    next_dev, prev_dev = (me + 1) & (TOK - 1), (me + TOK - 1) & (TOK - 1)

    def others(index):
        return [(index + k) & (LINE - 1) for k in (4, 3, 5, 2, 6, 1, 7)]

    steps = ((2, 0), (2, 1), (1, 0), (3, 0), (1, 1), (3, 1), (0, 1))
    along_x = [{"tok": ((x + i) & 3) * 8 + y_hi * 2 + (core ^ j)} for i, j in steps]
    along_y = [{"tok": x * 8 + (to >> 1) * 2 + core, "rep": (to & 1) * 8 + z} for to in others(y)]
    along_z = [(to, {"rep": y_lo * 8 + to}) for to in others(z)]
    barrier = pltpu.get_barrier_semaphore()

    def greet(dev):
        pl.semaphore_signal(barrier, inc=1, device_id=dev, device_id_type=MESH)

    for dev in [dev for _, dev in along_z] + along_y + along_x:
        greet(dev)
    outer = core * next_dev + (1 - core) * prev_dev
    greet({"tok": outer})
    sources = (key, query, value)
    load_rows = [
        pltpu.make_async_copy(src, cat.at[i, pl.ds(HALF, WIN)], local_sem.at[i]) for i, src in enumerate(sources)
    ]
    load_weight = pltpu.make_async_copy(weight, weight_v, local_sem.at[3])
    load_error = pltpu.make_async_copy(error_rows, error, local_sem.at[4])
    load_cot = pltpu.make_async_copy(cot_rows, cot_cat.at[pl.ds(HALF, WIN)], local_sem.at[5])
    for copy in [load_cot, load_error, *load_rows, load_weight]:
        copy.start()
    pl.semaphore_wait(barrier, 3 * (LINE - 1) + 1)

    def to_neighbours(i, first, second):
        copies = [
            pltpu.make_async_remote_copy(
                src, dst, halo_send.at[2 * i + j], halo_recv.at[2 * i + j], device_id={"tok": dev}, device_id_type=MESH
            )
            for j, (dev, (src, dst)) in enumerate(((prev_dev, first), (next_dev, second)))
        ]
        for copy in copies:
            copy.start()
        return copies

    def rows_to_neighbours(i, src, dst):
        return to_neighbours(
            i,
            (src.at[pl.ds(0, HALF)], dst.at[pl.ds(HALF + WIN, HALF)]),
            (src.at[pl.ds(HALF, HALF)], dst.at[pl.ds(0, HALF)]),
        )

    halo = [rows_to_neighbours(i, src, cat.at[i]) for i, src in enumerate(sources)]

    basis[...] = seeded_basis_t(seed[0])
    load_cot.wait()
    cot_basis[1] = mm_split(basis[...], cot_cat[HALF : HALF + WIN], NT)
    halo.append(to_neighbours(3, (cot_basis.at[1], cot_basis.at[2]), (cot_basis.at[1], cot_basis.at[0])))
    load_error.wait()
    mine = one_hot((RANK, WIDTH), lambda r, c: c == r + me * RANK)
    error_left[...] = mm_split(mm_exact(basis[...], error[...], NT), mine)

    def small(src, dst, sems, dev):
        send, recv = send_sem.at[sems], recv_sem.at[sems]
        pltpu.make_async_remote_copy(src, dst, send, recv, device_id=dev, device_id_type=MESH).start()

    def arrived(sem, ref):
        part = ref.at[pl.ds(1, LINE - 1)]
        pltpu.make_async_copy(part, part, sem).wait()

    def remote(src, dst, i, dev):
        return pltpu.make_async_remote_copy(
            src, dst, big_send.at[i], big_recv.at[i], device_id={"tok": dev}, device_id_type=MESH
        )

    def scatter(n, field):
        for i in range(LINE):
            chunks[n, i] = field[:, i * 128 : i * 128 + 128]
        for k, (to, dev) in enumerate(along_z):
            small(chunks.at[n, to], scat.at[n, 1 + k], 4 * n, dev)

    def line_send(n, line, total):
        index, devs = ((pair, along_x), (y, along_y))[line]
        sums[n, line, index] = total
        for dev in devs:
            small(sums.at[n, line, index], sums.at[n, line, index], 4 * n + 1 + line, dev)

    def line_sum(n, line):
        arrived(recv_sem.at[4 * n + 1 + line], sums.at[n, line])
        total = sums[n, line, 0]
        for j in range(1, LINE):
            total = total + sums[n, line, j]
        return total

    def sum_group(n):
        arrived(recv_sem.at[4 * n], scat.at[n])
        total = chunks[n, z]
        for k in range(1, LINE):
            total = total + scat[n, k]
        line_send(n, 0, total)

    def sum_first(n):
        line_send(n, 1, line_sum(n, 0))

    def sum_second(n):
        gath[n, z] = line_sum(n, 1) * (1.0 / REP)
        for _, dev in along_z:
            small(gath.at[n, z], gath.at[n, z], 4 * n + 3, dev)

    def gathered(n):
        arrived(recv_sem.at[4 * n + 3], gath.at[n])
        return jnp.concatenate([gath[n, i] for i in range(LINE)], 1)

    def sent(n):
        for i, ref in enumerate((scat.at[n], sums.at[n, 0], sums.at[n, 1], gath.at[n])):
            arrived(send_sem.at[4 * n + i], ref)

    offset = shift[0]
    start = jnp.where(offset <= HALF, offset + HALF, offset - HALF)
    pick = one_hot((WIN, 2 * WIN), lambda r, c: c == r + start)
    place = one_hot((2 * WIN, WIN), lambda r, c: r == c + start)
    head = lax.broadcasted_iota(jnp.int32, (WIN, 4 * HD), 1) // HD
    masks = [jnp.where(head == h, 1.0, 0.0).astype(BF16) for h in range(4)]

    def spread(a):
        return jnp.concatenate([a * mask for mask in masks], 0)

    def lanes(a):
        return jnp.concatenate([a[h] for h in range(4)], 1)

    def picked(i):
        load_rows[i].wait()
        for copy in halo[i]:
            copy.wait_recv()
        win[1 + i] = mm(pick, cat[i]).astype(BF16)

    picked(0)
    picked(1)
    cot_halo = rows_to_neighbours(4, cot_rows, cot_cat)
    for g in range(4):
        cols = slice(g * 256, g * 256 + 256)
        scores = (mm(spread(win[1, :, cols]), win[2, :, cols], NT) * 0.125).reshape(4, WIN, WIN)
        expo = jnp.exp(scores - jnp.max(scores, axis=1, keepdims=True))
        probs_s[g] = expo / jnp.sum(expo, axis=1, keepdims=True)
    picked(2)
    for g in range(4):
        cols = slice(g * 256, g * 256 + 256)
        low = probs_s[g].astype(BF16).reshape(4 * WIN, WIN)
        attn[:, cols] = mm(low, spread(win[3, :, cols]), TN).astype(BF16)

    for copy in halo[3]:
        copy.wait_recv()
    cot_cols = jnp.concatenate([cot_basis[i] for i in range(3)], 1)
    pick_cols = one_hot((3 * WIN, WIN), lambda r, c: r == c + start + HALF)
    part = mm_split(mm_split(cot_cols, pick_cols), attn[...]) * GRAD_SCALE + error_left[...]
    scatter(0, part)

    def send_back(i, arrays, cols):
        copies = [
            remote(outs.at[arrays, pl.ds(0, HALF), cols], ret_next.at[arrays, :, cols], i, prev_dev),
            remote(outs.at[arrays, pl.ds(HALF + WIN, HALF), cols], ret_prev.at[arrays, :, cols], i + 1, next_dev),
        ]
        for copy in copies:
            copy.start()
        return copies

    load_weight.wait()
    outs[0] = mm(place, mm(attn[...], weight_v[...]).astype(BF16)).astype(BF16)
    sum_group(0)
    for copy in cot_halo:
        copy.wait_recv()
    back = send_back(13, pl.ds(0, 1), pl.ds(0, WIDTH))
    cot = win.at[0]
    cot[...] = mm(pick, cot_cat[...]).astype(BF16)

    swaps = []
    for i, step in enumerate((2, 1, 3, 0)):
        to = (x + step) & 3
        cols = pl.ds(pl.multiple_of(to * 256, 256), 256)
        part = (mm(attn[:, cols], cot[...], TN) * GRAD_SCALE).reshape(4, 2, 32, WIDTH)
        blocks = pl.ds(4 * to, 4)
        grad[blocks] = jnp.where(core == 0, part[:, 0], part[:, 1])
        grad_low[blocks] = jnp.where(core == 0, part[:, 1], part[:, 0]).astype(BF16)
        swaps.append(remote(grad_low.at[blocks], recv_c.at[blocks], (0, 15, 16, 17)[i], me + 1 - 2 * core))
        swaps[-1].start()

    dattn[...] = mm(cot[...], weight_v[...], NT).astype(BF16)

    def backward(g):
        cols = slice(g * 256, g * 256 + 256)
        k4, q4, v4, d4 = win[1, :, cols], win[2, :, cols], win[3, :, cols], dattn[:, cols]
        probs = probs_s[g]
        low = probs.astype(BF16)
        dprob = mm(spread(v4), d4, NT).reshape(4, WIN, WIN)
        delta = jnp.sum(probs * dprob, axis=1, keepdims=True)
        dscore = (probs * (dprob - delta) * 0.125).astype(BF16)
        results = (
            mm(dscore.reshape(4 * WIN, WIN), spread(k4), TN),
            mm(lanes(dscore), spread(q4)),
            mm(lanes(low), spread(d4)),
        )
        for i, result in enumerate(results):
            outs[1 + i, :, cols] = mm(place, result.astype(BF16)).astype(BF16)

    def ring(index, count_dev, send, recv, first, part, ready):
        up, down, far = (index + 1) & 3, (index + 3) & 3, (index + 2) & 3
        to_up, to_down = count_dev(up), count_dev(down)
        copies = {
            (d, i): remote(send.at[d, i], recv.at[d, i], first + 3 * d + i, dev)
            for d, dev in enumerate((to_up, to_down))
            for i in range(3)
        }
        ready(0)
        for d in range(2):
            send[d, 0] = part(far, d).astype(BF16)
            copies[d, 0].start()

        def pure():
            for d, to in enumerate((up, down)):
                ready(1 + d)
                send[d, 1] = part(to, 1 - d).astype(BF16)
                copies[d, 1].start()

        def forward():
            for d, (to, rows) in enumerate(((up, 0), (down, 1))):
                copies[d, 0].wait_recv()
                send[d, 2] = (part(to, rows) + recv[d, 0].astype(F32)).astype(BF16)
                copies[d, 2].start()

        def total(rows):
            one, two = ((0, 2), (1, 1)) if rows == 0 else ((1, 2), (0, 1))
            return part(index, rows) + recv[one].astype(F32) + recv[two].astype(F32)

        def wait_total():
            ready(3)
            for d in range(2):
                copies[d, 1].wait_recv()
                copies[d, 2].wait_recv()

        return copies, pure, forward, wait_total, total

    def part_x(to, rows):
        blocks = pl.ds(4 * to + 2 * rows, 2)
        return grad[blocks] + recv_c[blocks].astype(F32)

    def part_y(to, rows):
        return mid[to, rows * 16 : rows * 16 + 16]

    backward(0)
    sum_first(0)
    copies_x, pure_x, forward_x, wait_x, total_x = ring(
        x, lambda to: to * 8 + y_hi * 2 + core, send_x, recv_x, 1, part_x, lambda i: swaps[i].wait_recv()
    )
    backward(1)
    backward(2)
    backward(3)
    pure_x()
    sum_second(0)
    forward_x()
    back += send_back(18, pl.ds(1, 3), pl.ds(0, WIDTH))

    left = gathered(0)
    left_mine = mm_split(left, mine, NT)
    attn_left = mm_split(left, attn[...], NT)
    part = mm_split(attn_left, cot[...]) * GRAD_SCALE
    scatter(1, part + mm_exact(left_mine, error[...]))

    rows = lax.broadcasted_iota(jnp.int32, (RANK, 1), 0)
    eye = lax.broadcasted_iota(jnp.int32, (RANK, RANK), 0) == lax.broadcasted_iota(jnp.int32, (RANK, RANK), 1)
    gram = mm_exact(left, left, NT)
    inverse = jnp.where(eye, 1.0, 0.0)
    for j in range(RANK - 1):
        factor = jnp.where(rows > j, gram[:, j : j + 1], 0.0) * (1.0 / gram[j : j + 1, j : j + 1])
        gram, inverse = gram - factor * gram[j : j + 1], inverse - factor * inverse[j : j + 1]
    pivots = jnp.sum(jnp.where(eye, gram, 0.0), axis=1, keepdims=True)
    inverse = inverse * (1.0 / jnp.sqrt(pivots))
    ortho_mine = mm_exact(inverse, left_mine)

    sum_group(1)
    wait_x()
    for rows in range(2):
        mid[2 * rows : 2 * rows + 2] = total_x(rows)
    copies_y, pure_y, forward_y, wait_y, total_y = ring(
        y_hi, lambda to: x * 8 + to * 2 + core, send_y, recv_y, 7, part_y, lambda i: None
    )
    pure_y()
    sum_first(1)
    sum_second(1)
    forward_y()

    for copy in back:
        copy.wait_recv()
    for i, out in enumerate((projected, qgrad, kgrad, vgrad)):
        out[0:HALF] = outs[i, HALF:WIN] + ret_prev[i]
        out[HALF:WIN] = outs[i, WIN : WIN + HALF] + ret_next[i]

    product = gathered(1)
    basis_t = mm_exact(inverse, product)
    low_rank = mm_exact(ortho_mine, basis_t, TN)
    update[...] = low_rank
    new_basis[...] = basis_t
    wait_y()
    for rows in range(2):
        at = slice(rows * 16, rows * 16 + 16)
        new_error[at] = total_y(rows) + error[at] - low_rank[at]

    for n in range(2):
        sent(n)
    for copy in [*swaps, *copies_x.values(), *copies_y.values(), *back, *cot_halo, *sum(halo, [])]:
        copy.wait_send()


def place_kernel(*refs):
    count = len(refs) // 2
    sems = refs[-1]
    copies = [pltpu.make_async_copy(refs[i], refs[count + i], sems.at[i]) for i in range(count)]
    for copy in copies:
        copy.start()
    for copy in copies:
        copy.wait()


def stay(array):
    return pltpu.with_memory_space_constraint(array, pltpu.HBM)


def body(
    query_rows, key_rows, value_rows, cotangent, out_weight, error_rows, window_shift, basis_seed
):
    smem = pl.BlockSpec(memory_space=pltpu.SMEM)
    vmem = pl.BlockSpec(memory_space=pltpu.VMEM)
    hbm = pl.BlockSpec(memory_space=pltpu.HBM)
    square = jax.ShapeDtypeStruct((RANK, WIDTH), F32)
    rows = jax.ShapeDtypeStruct((WIN, WIDTH), BF16)
    results = (rows,) * 4 + (square,) * 3
    parts = pl.pallas_call(
        main_kernel,
        out_shape=results,
        in_specs=[smem] * 2 + [hbm] * 6,
        out_specs=(vmem,) * 7,
        scratch_shapes=[
            pltpu.VMEM((3, 2 * WIN, WIDTH), BF16),
            pltpu.VMEM((3, RANK, WIN), F32),
            pltpu.VMEM((RANK, WIDTH), F32),
            pltpu.VMEM((RANK, WIDTH), F32),
            pltpu.VMEM((WIDTH, WIDTH), BF16),
            pltpu.VMEM((RANK, WIDTH), F32),
            pltpu.VMEM((2 * WIN, WIDTH), BF16),
            pltpu.VMEM((4, WIN, WIDTH), BF16),
            pltpu.VMEM((WIN, WIDTH), BF16),
            pltpu.VMEM((WIN, WIDTH), BF16),
            pltpu.VMEM((4, 4, WIN, WIN), F32),
            pltpu.VMEM((4, 2 * WIN, WIDTH), BF16),
            pltpu.VMEM((16, RANK, WIDTH), F32),
            pltpu.VMEM((16, RANK, WIDTH), BF16),
            pltpu.VMEM((16, RANK, WIDTH), BF16),
            pltpu.VMEM((2, 3, 2, RANK, WIDTH), BF16),
            pltpu.VMEM((2, 3, 2, RANK, WIDTH), BF16),
            pltpu.VMEM((4, RANK, WIDTH), F32),
            pltpu.VMEM((2, 3, 16, WIDTH), BF16),
            pltpu.VMEM((2, 3, 16, WIDTH), BF16),
            pltpu.VMEM((4, HALF, WIDTH), BF16),
            pltpu.VMEM((4, HALF, WIDTH), BF16),
            pltpu.VMEM((2, LINE, RANK, 128), F32),
            pltpu.VMEM((2, LINE, RANK, 128), F32),
            pltpu.VMEM((2, 2, LINE, RANK, 128), F32),
            pltpu.VMEM((2, LINE, RANK, 128), F32),
            pltpu.SemaphoreType.DMA((8,)),
            pltpu.SemaphoreType.DMA((8,)),
            pltpu.SemaphoreType.DMA((22,)),
            pltpu.SemaphoreType.DMA((22,)),
            pltpu.SemaphoreType.DMA((10,)),
            pltpu.SemaphoreType.DMA((10,)),
            pltpu.SemaphoreType.DMA((6,)),
        ],
        compiler_params=pltpu.CompilerParams(
            collective_id=0, has_side_effects=True, vmem_limit_bytes=32 * 2**20
        ),
        name="main",
    )(
        basis_seed,
        window_shift,
        *(stay(a[0]) for a in (query_rows, key_rows, value_rows, cotangent)),
        stay(out_weight),
        stay(error_rows[0]),
    )
    projected, qgrad, kgrad, vgrad, update, new_error, new_basis = pl.pallas_call(
        place_kernel,
        out_shape=results,
        in_specs=[vmem] * 7,
        out_specs=(hbm,) * 7,
        scratch_shapes=[pltpu.SemaphoreType.DMA((7,))],
        compiler_params=pltpu.CompilerParams(vmem_limit_bytes=8 * 2**20),
        name="place",
    )(*parts)
    return (
        projected[None],
        qgrad[None],
        kgrad[None],
        vgrad[None],
        update,
        new_error[None],
        new_basis.T,
    )


def solution(mesh):
    return jax.shard_map(
        body,
        mesh=mesh,
        in_specs=(
            P("rep", "tok", None),
            P("rep", "tok", None),
            P("rep", "tok", None),
            P("rep", "tok", None),
            P(),
            P("rep", "tok", None),
            P("rep"),
            P(),
        ),
        out_specs=(
            P("rep", "tok", None),
            P("rep", "tok", None),
            P("rep", "tok", None),
            P("rep", "tok", None),
            P("tok", None),
            P("rep", "tok", None),
            P(),
        ),
        check_vma=False,
    )
```

```python
import math

import jax
import jax.numpy as jnp
from jax import lax
from jax.experimental import pallas as pl
from jax.experimental.pallas import tpu as pltpu
from jax.sharding import PartitionSpec as P

H = 16
HD = 64
WIN = 128
HALF = 64
RANK = 32
WIDTH = 1024
TOK = 32
REP = 16
LINE = 8
PRIME = 65521
GRAD_SCALE = 1.0 / 64.0
F32 = jnp.float32
BF16 = jnp.bfloat16
MESH = pl.DeviceIdType.MESH
HIGHEST = lax.Precision.HIGHEST
NN = (((1,), (0,)), ((), ()))
NT = (((1,), (1,)), ((), ()))
TN = (((0,), (0,)), ((), ()))


def mod_prime(a):
    rest = a - (a.astype(F32) * (1.0 / PRIME)).astype(jnp.int32) * PRIME
    rest = jnp.where(rest < 0, rest + PRIME, rest)
    return jnp.where(rest >= PRIME, rest - PRIME, rest)


def seeded_basis_t(seed_value):
    row_index = lax.broadcasted_iota(jnp.int32, (RANK, WIDTH), 1)
    col_index = lax.broadcasted_iota(jnp.int32, (RANK, WIDTH), 0)
    mixed = mod_prime(row_index * 7919 + col_index * 31337 + (seed_value * 17 + 12345))
    mixed = mod_prime(mixed * 3877 + 29)
    mixed = mod_prime(mixed * 2011 + 7)
    return mixed.astype(F32) / 65521.0 - 0.5


def mm(a, b, dims=NN):
    return lax.dot_general(a, b, dims, preferred_element_type=F32)


def mm_exact(a, b, dims=NN):
    return lax.dot_general(a, b, dims, precision=HIGHEST, preferred_element_type=F32)


def mm_split(a, b, dims=NN):
    high = a.astype(BF16)
    rest = a - high.astype(F32)
    middle = rest.astype(BF16)
    low = (rest - middle.astype(F32)).astype(BF16)
    out = mm(jnp.concatenate([high, middle, low], 0), b, dims)
    return (out[2 * RANK :] + out[RANK : 2 * RANK]) + out[:RANK]


def one_hot(shape, row_to_col):
    rows = lax.broadcasted_iota(jnp.int32, shape, 0)
    cols = lax.broadcasted_iota(jnp.int32, shape, 1)
    return jnp.where(row_to_col(rows, cols), 1.0, 0.0).astype(BF16)


def main_kernel(
    seed, shift, query, key, value, cot_rows, weight, error_rows,
    projected, qgrad, kgrad, vgrad, update, new_error, new_basis,
    cat, cot_basis, basis, error_left, weight_v, error, cot_cat, win, dattn, attn, probs_s, outs, grad, grad_low, recv_c, send_x, recv_x, mid, send_y, recv_y,
    ret_prev, ret_next, chunks, scat, sums, gath, inverse_s, ortho_s,
    send_sem, recv_sem, big_send, big_recv, halo_send, halo_recv, local_sem,
):
    me = lax.axis_index("tok")
    rep = lax.axis_index("rep")
    core, y_hi, x = me & 1, (me >> 1) & 3, me >> 3
    y_lo, z = rep >> 3, rep & 7
    pair = x * 2 + core
    y = y_hi * 2 + y_lo
    next_dev, prev_dev = (me + 1) & (TOK - 1), (me + TOK - 1) & (TOK - 1)

    def others(index):
        return [(index + k) & (LINE - 1) for k in (4, 3, 5, 2, 6, 1, 7)]

    steps = ((2, 0), (2, 1), (1, 0), (3, 0), (1, 1), (3, 1), (0, 1))
    along_x = [{"tok": ((x + i) & 3) * 8 + y_hi * 2 + (core ^ j)} for i, j in steps]
    along_y = [{"tok": x * 8 + (to >> 1) * 2 + core, "rep": (to & 1) * 8 + z} for to in others(y)]
    along_z = [(to, {"rep": y_lo * 8 + to}) for to in others(z)]
    barrier = pltpu.get_barrier_semaphore()

    def greet(dev):
        pl.semaphore_signal(barrier, inc=1, device_id=dev, device_id_type=MESH)

    for dev in [dev for _, dev in along_z] + along_y + along_x:
        greet(dev)
    outer = core * next_dev + (1 - core) * prev_dev
    greet({"tok": outer})
    sources = (key, query, value)
    load_rows = [
        pltpu.make_async_copy(src, cat.at[i, pl.ds(HALF, WIN)], local_sem.at[i]) for i, src in enumerate(sources)
    ]
    load_weight = pltpu.make_async_copy(weight, weight_v, local_sem.at[3])
    load_error = pltpu.make_async_copy(error_rows, error, local_sem.at[4])
    load_cot = pltpu.make_async_copy(cot_rows, cot_cat.at[pl.ds(HALF, WIN)], local_sem.at[5])
    for copy in [load_cot, load_error, *load_rows, load_weight]:
        copy.start()
    pl.semaphore_wait(barrier, 3 * (LINE - 1) + 1)

    def to_neighbours(i, first, second):
        copies = [
            pltpu.make_async_remote_copy(
                src, dst, halo_send.at[2 * i + j], halo_recv.at[2 * i + j], device_id={"tok": dev}, device_id_type=MESH
            )
            for j, (dev, (src, dst)) in enumerate(((prev_dev, first), (next_dev, second)))
        ]
        for copy in copies:
            copy.start()
        return copies

    def rows_to_neighbours(i, src, dst):
        return to_neighbours(
            i,
            (src.at[pl.ds(0, HALF)], dst.at[pl.ds(HALF + WIN, HALF)]),
            (src.at[pl.ds(HALF, HALF)], dst.at[pl.ds(0, HALF)]),
        )

    halo = [rows_to_neighbours(i, src, cat.at[i]) for i, src in enumerate(sources)]

    basis[...] = seeded_basis_t(seed[0])
    load_cot.wait()
    cot_basis[1] = mm_split(basis[...], cot_cat[HALF : HALF + WIN], NT)
    halo.append(to_neighbours(3, (cot_basis.at[1], cot_basis.at[2]), (cot_basis.at[1], cot_basis.at[0])))
    load_error.wait()
    mine = one_hot((RANK, WIDTH), lambda r, c: c == r + me * RANK)
    error_left[...] = mm_split(mm_exact(basis[...], error[...], NT), mine)

    def small(src, dst, sems, dev):
        send, recv = send_sem.at[sems], recv_sem.at[sems]
        pltpu.make_async_remote_copy(src, dst, send, recv, device_id=dev, device_id_type=MESH).start()

    def arrived(sem, ref):
        part = ref.at[pl.ds(1, LINE - 1)]
        pltpu.make_async_copy(part, part, sem).wait()

    def remote(src, dst, i, dev):
        return pltpu.make_async_remote_copy(
            src, dst, big_send.at[i], big_recv.at[i], device_id={"tok": dev}, device_id_type=MESH
        )

    def scatter(n, field):
        for i in range(LINE):
            chunks[n, i] = field[:, i * 128 : i * 128 + 128]
        for k, (to, dev) in enumerate(along_z):
            small(chunks.at[n, to], scat.at[n, 1 + k], 4 * n, dev)

    def line_send(n, line, total):
        index, devs = ((pair, along_x), (y, along_y))[line]
        sums[n, line, index] = total
        for dev in devs:
            small(sums.at[n, line, index], sums.at[n, line, index], 4 * n + 1 + line, dev)

    def line_sum(n, line):
        arrived(recv_sem.at[4 * n + 1 + line], sums.at[n, line])
        total = sums[n, line, 0]
        for j in range(1, LINE):
            total = total + sums[n, line, j]
        return total

    def sum_group(n):
        arrived(recv_sem.at[4 * n], scat.at[n])
        total = chunks[n, z]
        for k in range(1, LINE):
            total = total + scat[n, k]
        line_send(n, 0, total)

    def sum_first(n):
        line_send(n, 1, line_sum(n, 0))

    def sum_second(n):
        gath[n, z] = line_sum(n, 1) * (1.0 / REP)
        for _, dev in along_z:
            small(gath.at[n, z], gath.at[n, z], 4 * n + 3, dev)

    def gathered(n):
        arrived(recv_sem.at[4 * n + 3], gath.at[n])
        return jnp.concatenate([gath[n, i] for i in range(LINE)], 1)

    def sent(n):
        for i, ref in enumerate((scat.at[n], sums.at[n, 0], sums.at[n, 1], gath.at[n])):
            arrived(send_sem.at[4 * n + i], ref)

    offset = shift[0]
    start = jnp.where(offset <= HALF, offset + HALF, offset - HALF)
    pick = one_hot((WIN, 2 * WIN), lambda r, c: c == r + start)
    place = one_hot((2 * WIN, WIN), lambda r, c: r == c + start)
    head = lax.broadcasted_iota(jnp.int32, (WIN, 4 * HD), 1) // HD
    masks = [jnp.where(head == h, 1.0, 0.0).astype(BF16) for h in range(4)]

    def spread(a):
        return jnp.concatenate([a * mask for mask in masks], 0)

    def lanes(a):
        return jnp.concatenate([a[h] for h in range(4)], 1)

    def picked(i):
        load_rows[i].wait()
        for copy in halo[i]:
            copy.wait_recv()
        win[1 + i] = mm(pick, cat[i]).astype(BF16)

    picked(0)
    picked(1)
    cot_halo = rows_to_neighbours(4, cot_rows, cot_cat)
    for g in range(4):
        cols = slice(g * 256, g * 256 + 256)
        scores = (mm(spread(win[1, :, cols]), win[2, :, cols], NT) * 0.125).reshape(4, WIN, WIN)
        expo = jnp.exp(scores - jnp.max(scores, axis=1, keepdims=True))
        probs_s[g] = expo / jnp.sum(expo, axis=1, keepdims=True)
    picked(2)
    for g in range(4):
        cols = slice(g * 256, g * 256 + 256)
        low = probs_s[g].astype(BF16).reshape(4 * WIN, WIN)
        attn[:, cols] = mm(low, spread(win[3, :, cols]), TN).astype(BF16)

    for copy in halo[3]:
        copy.wait_recv()
    cot_cols = jnp.concatenate([cot_basis[i] for i in range(3)], 1)
    pick_cols = one_hot((3 * WIN, WIN), lambda r, c: r == c + start + HALF)
    part = mm_split(mm_split(cot_cols, pick_cols), attn[...]) * GRAD_SCALE + error_left[...]
    scatter(0, part)

    def send_back(i, arrays, cols):
        copies = [
            remote(outs.at[arrays, pl.ds(0, HALF), cols], ret_next.at[arrays, :, cols], i, prev_dev),
            remote(outs.at[arrays, pl.ds(HALF + WIN, HALF), cols], ret_prev.at[arrays, :, cols], i + 1, next_dev),
        ]
        for copy in copies:
            copy.start()
        return copies

    load_weight.wait()
    outs[0] = mm(place, mm(attn[...], weight_v[...]).astype(BF16)).astype(BF16)
    sum_group(0)
    for copy in cot_halo:
        copy.wait_recv()
    back = send_back(13, pl.ds(0, 1), pl.ds(0, WIDTH))
    cot = win.at[0]
    cot[...] = mm(pick, cot_cat[...]).astype(BF16)

    swaps = []
    for i, step in enumerate((2, 1, 3, 0)):
        to = (x + step) & 3
        cols = pl.ds(pl.multiple_of(to * 256, 256), 256)
        part = (mm(attn[:, cols], cot[...], TN) * GRAD_SCALE).reshape(4, 2, 32, WIDTH)
        blocks = pl.ds(4 * to, 4)
        grad[blocks] = jnp.where(core == 0, part[:, 0], part[:, 1])
        grad_low[blocks] = jnp.where(core == 0, part[:, 1], part[:, 0]).astype(BF16)
        swaps.append(remote(grad_low.at[blocks], recv_c.at[blocks], (0, 15, 16, 17)[i], me + 1 - 2 * core))
        swaps[-1].start()

    dattn[...] = mm(cot[...], weight_v[...], NT).astype(BF16)

    def backward(g):
        cols = slice(g * 256, g * 256 + 256)
        k4, q4, v4, d4 = win[1, :, cols], win[2, :, cols], win[3, :, cols], dattn[:, cols]
        probs = probs_s[g]
        low = probs.astype(BF16)
        dprob = mm(spread(v4), d4, NT).reshape(4, WIN, WIN)
        delta = jnp.sum(probs * dprob, axis=1, keepdims=True)
        dscore = (probs * (dprob - delta) * 0.125).astype(BF16)
        results = (
            mm(dscore.reshape(4 * WIN, WIN), spread(k4), TN),
            mm(lanes(dscore), spread(q4)),
            mm(lanes(low), spread(d4)),
        )
        for i, result in enumerate(results):
            outs[1 + i, :, cols] = mm(place, result.astype(BF16)).astype(BF16)

    def ring(index, count_dev, send, recv, first, part, ready):
        up, down, far = (index + 1) & 3, (index + 3) & 3, (index + 2) & 3
        to_up, to_down = count_dev(up), count_dev(down)
        copies = {
            (d, i): remote(send.at[d, i], recv.at[d, i], first + 3 * d + i, dev)
            for d, dev in enumerate((to_up, to_down))
            for i in range(3)
        }
        ready(0)
        for d in range(2):
            send[d, 0] = part(far, d).astype(BF16)
            copies[d, 0].start()

        def pure():
            for d, to in enumerate((up, down)):
                ready(1 + d)
                send[d, 1] = part(to, 1 - d).astype(BF16)
                copies[d, 1].start()

        def forward():
            for d, (to, rows) in enumerate(((up, 0), (down, 1))):
                copies[d, 0].wait_recv()
                send[d, 2] = (part(to, rows) + recv[d, 0].astype(F32)).astype(BF16)
                copies[d, 2].start()

        def total(rows):
            one, two = ((0, 2), (1, 1)) if rows == 0 else ((1, 2), (0, 1))
            return part(index, rows) + recv[one].astype(F32) + recv[two].astype(F32)

        def wait_total():
            ready(3)
            for d in range(2):
                copies[d, 1].wait_recv()
                copies[d, 2].wait_recv()

        return copies, pure, forward, wait_total, total

    def part_x(to, rows):
        blocks = pl.ds(4 * to + 2 * rows, 2)
        return grad[blocks] + recv_c[blocks].astype(F32)

    def part_y(to, rows):
        return mid[to, rows * 16 : rows * 16 + 16]

    backward(0)
    sum_first(0)
    copies_x, pure_x, forward_x, wait_x, total_x = ring(
        x, lambda to: to * 8 + y_hi * 2 + core, send_x, recv_x, 1, part_x, lambda i: swaps[i].wait_recv()
    )
    backward(1)
    backward(2)
    backward(3)
    pure_x()
    sum_second(0)
    forward_x()
    back += send_back(18, pl.ds(1, 3), pl.ds(0, WIDTH))

    left = gathered(0)
    left_mine = mm_split(left, mine, NT)
    attn_left = mm_split(left, attn[...], NT)
    part = mm_split(attn_left, cot[...]) * GRAD_SCALE
    scatter(1, part + mm_exact(left_mine, error[...]))

    @pl.when(me >= 0)
    def _():
        rows = lax.broadcasted_iota(jnp.int32, (RANK, 1), 0)
        eye = lax.broadcasted_iota(jnp.int32, (RANK, RANK), 0) == lax.broadcasted_iota(jnp.int32, (RANK, RANK), 1)
        gram = mm_exact(left, left, NT)
        inverse = jnp.where(eye, 1.0, 0.0)
        for j in range(RANK - 1):
            factor = jnp.where(rows > j, gram[:, j : j + 1], 0.0) * (1.0 / gram[j : j + 1, j : j + 1])
            gram, inverse = gram - factor * gram[j : j + 1], inverse - factor * inverse[j : j + 1]
        pivots = jnp.sum(jnp.where(eye, gram, 0.0), axis=1, keepdims=True)
        inverse = inverse * (1.0 / jnp.sqrt(pivots))
        ortho_s[...] = mm_exact(inverse, left_mine)
        inverse_s[...] = inverse

    sum_group(1)
    wait_x()
    for rows in range(2):
        mid[2 * rows : 2 * rows + 2] = total_x(rows)
    copies_y, pure_y, forward_y, wait_y, total_y = ring(
        y_hi, lambda to: x * 8 + to * 2 + core, send_y, recv_y, 7, part_y, lambda i: None
    )
    pure_y()
    sum_first(1)
    sum_second(1)
    forward_y()

    for copy in back:
        copy.wait_recv()
    for i, out in enumerate((projected, qgrad, kgrad, vgrad)):
        out[0:HALF] = outs[i, HALF:WIN] + ret_prev[i]
        out[HALF:WIN] = outs[i, WIN : WIN + HALF] + ret_next[i]

    product = gathered(1)
    basis_t = mm_exact(inverse_s[...], product)
    low_rank = mm_exact(ortho_s[...], basis_t, TN)
    update[...] = low_rank
    new_basis[...] = basis_t
    wait_y()
    for rows in range(2):
        at = slice(rows * 16, rows * 16 + 16)
        new_error[at] = total_y(rows) + error[at] - low_rank[at]

    for n in range(2):
        sent(n)
    for copy in [*swaps, *copies_x.values(), *copies_y.values(), *back, *cot_halo, *sum(halo, [])]:
        copy.wait_send()


def place_kernel(*refs):
    count = len(refs) // 2
    sems = refs[-1]
    copies = [pltpu.make_async_copy(refs[i], refs[count + i], sems.at[i]) for i in range(count)]
    for copy in copies:
        copy.start()
    for copy in copies:
        copy.wait()


def stay(array):
    return pltpu.with_memory_space_constraint(array, pltpu.HBM)


def body(
    query_rows, key_rows, value_rows, cotangent, out_weight, error_rows, window_shift, basis_seed
):
    smem = pl.BlockSpec(memory_space=pltpu.SMEM)
    vmem = pl.BlockSpec(memory_space=pltpu.VMEM)
    hbm = pl.BlockSpec(memory_space=pltpu.HBM)
    square = jax.ShapeDtypeStruct((RANK, WIDTH), F32)
    rows = jax.ShapeDtypeStruct((WIN, WIDTH), BF16)
    results = (rows,) * 4 + (square,) * 3
    parts = pl.pallas_call(
        main_kernel,
        out_shape=results,
        in_specs=[smem] * 2 + [hbm] * 6,
        out_specs=(vmem,) * 7,
        scratch_shapes=[
            pltpu.VMEM((3, 2 * WIN, WIDTH), BF16),
            pltpu.VMEM((3, RANK, WIN), F32),
            pltpu.VMEM((RANK, WIDTH), F32),
            pltpu.VMEM((RANK, WIDTH), F32),
            pltpu.VMEM((WIDTH, WIDTH), BF16),
            pltpu.VMEM((RANK, WIDTH), F32),
            pltpu.VMEM((2 * WIN, WIDTH), BF16),
            pltpu.VMEM((4, WIN, WIDTH), BF16),
            pltpu.VMEM((WIN, WIDTH), BF16),
            pltpu.VMEM((WIN, WIDTH), BF16),
            pltpu.VMEM((4, 4, WIN, WIN), F32),
            pltpu.VMEM((4, 2 * WIN, WIDTH), BF16),
            pltpu.VMEM((16, RANK, WIDTH), F32),
            pltpu.VMEM((16, RANK, WIDTH), BF16),
            pltpu.VMEM((16, RANK, WIDTH), BF16),
            pltpu.VMEM((2, 3, 2, RANK, WIDTH), BF16),
            pltpu.VMEM((2, 3, 2, RANK, WIDTH), BF16),
            pltpu.VMEM((4, RANK, WIDTH), F32),
            pltpu.VMEM((2, 3, 16, WIDTH), BF16),
            pltpu.VMEM((2, 3, 16, WIDTH), BF16),
            pltpu.VMEM((4, HALF, WIDTH), BF16),
            pltpu.VMEM((4, HALF, WIDTH), BF16),
            pltpu.VMEM((2, LINE, RANK, 128), F32),
            pltpu.VMEM((2, LINE, RANK, 128), F32),
            pltpu.VMEM((2, 2, LINE, RANK, 128), F32),
            pltpu.VMEM((2, LINE, RANK, 128), F32),
            pltpu.VMEM((RANK, RANK), F32),
            pltpu.VMEM((RANK, RANK), F32),
            pltpu.SemaphoreType.DMA((8,)),
            pltpu.SemaphoreType.DMA((8,)),
            pltpu.SemaphoreType.DMA((22,)),
            pltpu.SemaphoreType.DMA((22,)),
            pltpu.SemaphoreType.DMA((10,)),
            pltpu.SemaphoreType.DMA((10,)),
            pltpu.SemaphoreType.DMA((6,)),
        ],
        compiler_params=pltpu.CompilerParams(
            collective_id=0, has_side_effects=True, vmem_limit_bytes=32 * 2**20
        ),
        name="main",
    )(
        basis_seed,
        window_shift,
        *(stay(a[0]) for a in (query_rows, key_rows, value_rows, cotangent)),
        stay(out_weight),
        stay(error_rows[0]),
    )
    projected, qgrad, kgrad, vgrad, update, new_error, new_basis = pl.pallas_call(
        place_kernel,
        out_shape=results,
        in_specs=[vmem] * 7,
        out_specs=(hbm,) * 7,
        scratch_shapes=[pltpu.SemaphoreType.DMA((7,))],
        compiler_params=pltpu.CompilerParams(vmem_limit_bytes=8 * 2**20),
        name="place",
    )(*parts)
    return (
        projected[None],
        qgrad[None],
        kgrad[None],
        vgrad[None],
        update,
        new_error[None],
        new_basis.T,
    )


def solution(mesh):
    return jax.shard_map(
        body,
        mesh=mesh,
        in_specs=(
            P("rep", "tok", None),
            P("rep", "tok", None),
            P("rep", "tok", None),
            P("rep", "tok", None),
            P(),
            P("rep", "tok", None),
            P("rep"),
            P(),
        ),
        out_specs=(
            P("rep", "tok", None),
            P("rep", "tok", None),
            P("rep", "tok", None),
            P("rep", "tok", None),
            P("tok", None),
            P("rep", "tok", None),
            P(),
        ),
        check_vma=False,
    )
```

```python
import math

import jax
import jax.numpy as jnp
from jax import lax
from jax.experimental import pallas as pl
from jax.experimental.pallas import tpu as pltpu
from jax.sharding import PartitionSpec as P

H = 16
HD = 64
WIN = 128
HALF = 64
RANK = 32
WIDTH = 1024
TOK = 32
REP = 16
LINE = 8
PRIME = 65521
GRAD_SCALE = 1.0 / 64.0
F32 = jnp.float32
BF16 = jnp.bfloat16
MESH = pl.DeviceIdType.MESH
HIGHEST = lax.Precision.HIGHEST
NN = (((1,), (0,)), ((), ()))
NT = (((1,), (1,)), ((), ()))
TN = (((0,), (0,)), ((), ()))


def mod_prime(a):
    rest = a - (a.astype(F32) * (1.0 / PRIME)).astype(jnp.int32) * PRIME
    rest = jnp.where(rest < 0, rest + PRIME, rest)
    return jnp.where(rest >= PRIME, rest - PRIME, rest)


def seeded_basis_t(seed_value):
    row_index = lax.broadcasted_iota(jnp.int32, (RANK, WIDTH), 1)
    col_index = lax.broadcasted_iota(jnp.int32, (RANK, WIDTH), 0)
    mixed = mod_prime(row_index * 7919 + col_index * 31337 + (seed_value * 17 + 12345))
    mixed = mod_prime(mixed * 3877 + 29)
    mixed = mod_prime(mixed * 2011 + 7)
    return mixed.astype(F32) / 65521.0 - 0.5


def mm(a, b, dims=NN):
    return lax.dot_general(a, b, dims, preferred_element_type=F32)


def mm_exact(a, b, dims=NN):
    return lax.dot_general(a, b, dims, precision=HIGHEST, preferred_element_type=F32)


def mm_split(a, b, dims=NN):
    high = a.astype(BF16)
    rest = a - high.astype(F32)
    middle = rest.astype(BF16)
    low = (rest - middle.astype(F32)).astype(BF16)
    out = mm(jnp.concatenate([high, middle, low], 0), b, dims)
    return (out[2 * RANK :] + out[RANK : 2 * RANK]) + out[:RANK]


def one_hot(shape, row_to_col):
    rows = lax.broadcasted_iota(jnp.int32, shape, 0)
    cols = lax.broadcasted_iota(jnp.int32, shape, 1)
    return jnp.where(row_to_col(rows, cols), 1.0, 0.0).astype(BF16)


def main_kernel(
    seed, shift, query, key, value, cot_rows, weight, error_rows,
    projected, qgrad, kgrad, vgrad, update, new_error, new_basis,
    cat, cot_basis, basis, error_left, weight_v, error, cot_cat, win, dattn, attn, probs_s, outs, grad, grad_low, recv_c, send_x, recv_x, mid, send_y, recv_y,
    ret_prev, ret_next, chunks, scat, sums, gath, inverse_s, ortho_s,
    send_sem, recv_sem, big_send, big_recv, halo_send, halo_recv, local_sem,
):
    me = lax.axis_index("tok")
    rep = lax.axis_index("rep")
    core, y_hi, x = me & 1, (me >> 1) & 3, me >> 3
    y_lo, z = rep >> 3, rep & 7
    pair = x * 2 + core
    y = y_hi * 2 + y_lo
    next_dev, prev_dev = (me + 1) & (TOK - 1), (me + TOK - 1) & (TOK - 1)

    def others(index):
        return [(index + k) & (LINE - 1) for k in (4, 3, 5, 2, 6, 1, 7)]

    steps = ((2, 0), (2, 1), (1, 0), (3, 0), (1, 1), (3, 1), (0, 1))
    along_x = [{"tok": ((x + i) & 3) * 8 + y_hi * 2 + (core ^ j)} for i, j in steps]
    along_y = [{"tok": x * 8 + (to >> 1) * 2 + core, "rep": (to & 1) * 8 + z} for to in others(y)]
    along_z = [(to, {"rep": y_lo * 8 + to}) for to in others(z)]
    barrier = pltpu.get_barrier_semaphore()

    def greet(dev):
        pl.semaphore_signal(barrier, inc=1, device_id=dev, device_id_type=MESH)

    for dev in [dev for _, dev in along_z] + along_y + along_x:
        greet(dev)
    outer = core * next_dev + (1 - core) * prev_dev
    greet({"tok": outer})
    sources = (key, query, value)
    load_rows = [
        pltpu.make_async_copy(src, cat.at[i, pl.ds(HALF, WIN)], local_sem.at[i]) for i, src in enumerate(sources)
    ]
    load_weight = pltpu.make_async_copy(weight, weight_v, local_sem.at[3])
    load_error = pltpu.make_async_copy(error_rows, error, local_sem.at[4])
    load_cot = pltpu.make_async_copy(cot_rows, cot_cat.at[pl.ds(HALF, WIN)], local_sem.at[5])
    for copy in [load_cot, load_error, *load_rows, load_weight]:
        copy.start()
    pl.semaphore_wait(barrier, 3 * (LINE - 1) + 1)

    def to_neighbours(i, first, second):
        copies = [
            pltpu.make_async_remote_copy(
                src, dst, halo_send.at[2 * i + j], halo_recv.at[2 * i + j], device_id={"tok": dev}, device_id_type=MESH
            )
            for j, (dev, (src, dst)) in enumerate(((prev_dev, first), (next_dev, second)))
        ]
        for copy in copies:
            copy.start()
        return copies

    def rows_to_neighbours(i, src, dst):
        return to_neighbours(
            i,
            (src.at[pl.ds(0, HALF)], dst.at[pl.ds(HALF + WIN, HALF)]),
            (src.at[pl.ds(HALF, HALF)], dst.at[pl.ds(0, HALF)]),
        )

    halo = [rows_to_neighbours(i, src, cat.at[i]) for i, src in enumerate(sources)]

    basis[...] = seeded_basis_t(seed[0])
    load_cot.wait()
    cot_basis[1] = mm_split(basis[...], cot_cat[HALF : HALF + WIN], NT)
    halo.append(to_neighbours(3, (cot_basis.at[1], cot_basis.at[2]), (cot_basis.at[1], cot_basis.at[0])))
    load_error.wait()
    mine = one_hot((RANK, WIDTH), lambda r, c: c == r + me * RANK)
    error_left[...] = mm_split(mm_exact(basis[...], error[...], NT), mine)

    def small(src, dst, sems, dev):
        send, recv = send_sem.at[sems], recv_sem.at[sems]
        pltpu.make_async_remote_copy(src, dst, send, recv, device_id=dev, device_id_type=MESH).start()

    def arrived(sem, ref):
        part = ref.at[pl.ds(1, LINE - 1)]
        pltpu.make_async_copy(part, part, sem).wait()

    def remote(src, dst, i, dev):
        return pltpu.make_async_remote_copy(
            src, dst, big_send.at[i], big_recv.at[i], device_id={"tok": dev}, device_id_type=MESH
        )

    def scatter(n, field):
        for i in range(LINE):
            chunks[n, i] = field[:, i * 128 : i * 128 + 128]
        for k, (to, dev) in enumerate(along_z):
            small(chunks.at[n, to], scat.at[n, 1 + k], 4 * n, dev)

    def line_send(n, line, total):
        index, devs = ((pair, along_x), (y, along_y))[line]
        sums[n, line, index] = total
        for dev in devs:
            small(sums.at[n, line, index], sums.at[n, line, index], 4 * n + 1 + line, dev)

    def line_sum(n, line):
        arrived(recv_sem.at[4 * n + 1 + line], sums.at[n, line])
        total = sums[n, line, 0]
        for j in range(1, LINE):
            total = total + sums[n, line, j]
        return total

    def sum_group(n):
        arrived(recv_sem.at[4 * n], scat.at[n])
        total = chunks[n, z]
        for k in range(1, LINE):
            total = total + scat[n, k]
        line_send(n, 0, total)

    def sum_first(n):
        line_send(n, 1, line_sum(n, 0))

    def sum_second(n):
        gath[n, z] = line_sum(n, 1) * (1.0 / REP)
        for _, dev in along_z:
            small(gath.at[n, z], gath.at[n, z], 4 * n + 3, dev)

    def gathered(n):
        arrived(recv_sem.at[4 * n + 3], gath.at[n])
        return jnp.concatenate([gath[n, i] for i in range(LINE)], 1)

    def sent(n):
        for i, ref in enumerate((scat.at[n], sums.at[n, 0], sums.at[n, 1], gath.at[n])):
            arrived(send_sem.at[4 * n + i], ref)

    offset = shift[0]
    start = jnp.where(offset <= HALF, offset + HALF, offset - HALF)
    pick = one_hot((WIN, 2 * WIN), lambda r, c: c == r + start)
    place = one_hot((2 * WIN, WIN), lambda r, c: r == c + start)
    head = lax.broadcasted_iota(jnp.int32, (WIN, 4 * HD), 1) // HD
    masks = [jnp.where(head == h, 1.0, 0.0).astype(BF16) for h in range(4)]

    def spread(a):
        return jnp.concatenate([a * mask for mask in masks], 0)

    def lanes(a):
        return jnp.concatenate([a[h] for h in range(4)], 1)

    def picked(i):
        load_rows[i].wait()
        for copy in halo[i]:
            copy.wait_recv()
        win[1 + i] = mm(pick, cat[i]).astype(BF16)

    picked(0)
    picked(1)
    cot_halo = rows_to_neighbours(4, cot_rows, cot_cat)
    for g in range(4):
        cols = slice(g * 256, g * 256 + 256)
        scores = (mm(spread(win[1, :, cols]), win[2, :, cols], NT) * 0.125).reshape(4, WIN, WIN)
        expo = jnp.exp(scores - jnp.max(scores, axis=1, keepdims=True))
        probs_s[g] = expo / jnp.sum(expo, axis=1, keepdims=True)
    picked(2)
    for g in range(4):
        cols = slice(g * 256, g * 256 + 256)
        low = probs_s[g].astype(BF16).reshape(4 * WIN, WIN)
        attn[:, cols] = mm(low, spread(win[3, :, cols]), TN).astype(BF16)

    for copy in halo[3]:
        copy.wait_recv()
    cot_cols = jnp.concatenate([cot_basis[i] for i in range(3)], 1)
    pick_cols = one_hot((3 * WIN, WIN), lambda r, c: r == c + start + HALF)
    part = mm_split(mm_split(cot_cols, pick_cols), attn[...]) * GRAD_SCALE + error_left[...]
    scatter(0, part)

    def send_back(i, arrays, cols):
        copies = [
            remote(outs.at[arrays, pl.ds(0, HALF), cols], ret_next.at[arrays, :, cols], i, prev_dev),
            remote(outs.at[arrays, pl.ds(HALF + WIN, HALF), cols], ret_prev.at[arrays, :, cols], i + 1, next_dev),
        ]
        for copy in copies:
            copy.start()
        return copies

    load_weight.wait()

    @pl.when(me >= 0)
    def _():
        outs[0] = mm(place, mm(attn[...], weight_v[...]).astype(BF16)).astype(BF16)

    sum_group(0)
    for copy in cot_halo:
        copy.wait_recv()
    back = send_back(13, pl.ds(0, 1), pl.ds(0, WIDTH))
    cot = win.at[0]
    cot[...] = mm(pick, cot_cat[...]).astype(BF16)

    swaps = []
    for i, step in enumerate((2, 1, 3, 0)):
        to = (x + step) & 3
        cols = pl.ds(pl.multiple_of(to * 256, 256), 256)
        part = (mm(attn[:, cols], cot[...], TN) * GRAD_SCALE).reshape(4, 2, 32, WIDTH)
        blocks = pl.ds(4 * to, 4)
        grad[blocks] = jnp.where(core == 0, part[:, 0], part[:, 1])
        grad_low[blocks] = jnp.where(core == 0, part[:, 1], part[:, 0]).astype(BF16)
        swaps.append(remote(grad_low.at[blocks], recv_c.at[blocks], (0, 15, 16, 17)[i], me + 1 - 2 * core))
        swaps[-1].start()

    dattn[...] = mm(cot[...], weight_v[...], NT).astype(BF16)

    def backward(g):
        cols = slice(g * 256, g * 256 + 256)
        k4, q4, v4, d4 = win[1, :, cols], win[2, :, cols], win[3, :, cols], dattn[:, cols]
        probs = probs_s[g]
        low = probs.astype(BF16)
        dprob = mm(spread(v4), d4, NT).reshape(4, WIN, WIN)
        delta = jnp.sum(probs * dprob, axis=1, keepdims=True)
        dscore = (probs * (dprob - delta) * 0.125).astype(BF16)
        results = (
            mm(dscore.reshape(4 * WIN, WIN), spread(k4), TN),
            mm(lanes(dscore), spread(q4)),
            mm(lanes(low), spread(d4)),
        )
        for i, result in enumerate(results):
            outs[1 + i, :, cols] = mm(place, result.astype(BF16)).astype(BF16)

    def ring(index, count_dev, send, recv, first, part, ready):
        up, down, far = (index + 1) & 3, (index + 3) & 3, (index + 2) & 3
        to_up, to_down = count_dev(up), count_dev(down)
        copies = {
            (d, i): remote(send.at[d, i], recv.at[d, i], first + 3 * d + i, dev)
            for d, dev in enumerate((to_up, to_down))
            for i in range(3)
        }
        ready(0)
        for d in range(2):
            send[d, 0] = part(far, d).astype(BF16)
            copies[d, 0].start()

        def pure():
            for d, to in enumerate((up, down)):
                ready(1 + d)
                send[d, 1] = part(to, 1 - d).astype(BF16)
                copies[d, 1].start()

        def forward():
            for d, (to, rows) in enumerate(((up, 0), (down, 1))):
                copies[d, 0].wait_recv()
                send[d, 2] = (part(to, rows) + recv[d, 0].astype(F32)).astype(BF16)
                copies[d, 2].start()

        def total(rows):
            one, two = ((0, 2), (1, 1)) if rows == 0 else ((1, 2), (0, 1))
            return part(index, rows) + recv[one].astype(F32) + recv[two].astype(F32)

        def wait_total():
            ready(3)
            for d in range(2):
                copies[d, 1].wait_recv()
                copies[d, 2].wait_recv()

        return copies, pure, forward, wait_total, total

    def part_x(to, rows):
        blocks = pl.ds(4 * to + 2 * rows, 2)
        return grad[blocks] + recv_c[blocks].astype(F32)

    def part_y(to, rows):
        return mid[to, rows * 16 : rows * 16 + 16]

    backward(0)
    sum_first(0)
    copies_x, pure_x, forward_x, wait_x, total_x = ring(
        x, lambda to: to * 8 + y_hi * 2 + core, send_x, recv_x, 1, part_x, lambda i: swaps[i].wait_recv()
    )
    backward(1)
    backward(2)
    backward(3)
    pure_x()
    sum_second(0)
    forward_x()
    back += send_back(18, pl.ds(1, 3), pl.ds(0, WIDTH))

    left = gathered(0)
    left_mine = mm_split(left, mine, NT)
    attn_left = mm_split(left, attn[...], NT)
    part = mm_split(attn_left, cot[...]) * GRAD_SCALE
    scatter(1, part + mm_exact(left_mine, error[...]))

    @pl.when(me >= 0)
    def _():
        rows = lax.broadcasted_iota(jnp.int32, (RANK, 1), 0)
        eye = lax.broadcasted_iota(jnp.int32, (RANK, RANK), 0) == lax.broadcasted_iota(jnp.int32, (RANK, RANK), 1)
        gram = mm_exact(left, left, NT)
        inverse = jnp.where(eye, 1.0, 0.0)
        for j in range(RANK - 1):
            factor = jnp.where(rows > j, gram[:, j : j + 1], 0.0) * (1.0 / gram[j : j + 1, j : j + 1])
            gram, inverse = gram - factor * gram[j : j + 1], inverse - factor * inverse[j : j + 1]
        pivots = jnp.sum(jnp.where(eye, gram, 0.0), axis=1, keepdims=True)
        inverse = inverse * (1.0 / jnp.sqrt(pivots))
        ortho_s[...] = mm_exact(inverse, left_mine)
        inverse_s[...] = inverse

    sum_group(1)
    wait_x()
    for rows in range(2):
        mid[2 * rows : 2 * rows + 2] = total_x(rows)
    copies_y, pure_y, forward_y, wait_y, total_y = ring(
        y_hi, lambda to: x * 8 + to * 2 + core, send_y, recv_y, 7, part_y, lambda i: None
    )
    pure_y()
    sum_first(1)
    sum_second(1)
    forward_y()

    for copy in back:
        copy.wait_recv()
    for i, out in enumerate((projected, qgrad, kgrad, vgrad)):
        out[0:HALF] = outs[i, HALF:WIN] + ret_prev[i]
        out[HALF:WIN] = outs[i, WIN : WIN + HALF] + ret_next[i]

    product = gathered(1)
    basis_t = mm_exact(inverse_s[...], product)
    low_rank = mm_exact(ortho_s[...], basis_t, TN)
    update[...] = low_rank
    new_basis[...] = basis_t
    wait_y()
    for rows in range(2):
        at = slice(rows * 16, rows * 16 + 16)
        new_error[at] = total_y(rows) + error[at] - low_rank[at]

    for n in range(2):
        sent(n)
    for copy in [*swaps, *copies_x.values(), *copies_y.values(), *back, *cot_halo, *sum(halo, [])]:
        copy.wait_send()


def place_kernel(*refs):
    count = len(refs) // 2
    sems = refs[-1]
    copies = [pltpu.make_async_copy(refs[i], refs[count + i], sems.at[i]) for i in range(count)]
    for copy in copies:
        copy.start()
    for copy in copies:
        copy.wait()


def stay(array):
    return pltpu.with_memory_space_constraint(array, pltpu.HBM)


def body(
    query_rows, key_rows, value_rows, cotangent, out_weight, error_rows, window_shift, basis_seed
):
    smem = pl.BlockSpec(memory_space=pltpu.SMEM)
    vmem = pl.BlockSpec(memory_space=pltpu.VMEM)
    hbm = pl.BlockSpec(memory_space=pltpu.HBM)
    square = jax.ShapeDtypeStruct((RANK, WIDTH), F32)
    rows = jax.ShapeDtypeStruct((WIN, WIDTH), BF16)
    results = (rows,) * 4 + (square,) * 3
    parts = pl.pallas_call(
        main_kernel,
        out_shape=results,
        in_specs=[smem] * 2 + [hbm] * 6,
        out_specs=(vmem,) * 7,
        scratch_shapes=[
            pltpu.VMEM((3, 2 * WIN, WIDTH), BF16),
            pltpu.VMEM((3, RANK, WIN), F32),
            pltpu.VMEM((RANK, WIDTH), F32),
            pltpu.VMEM((RANK, WIDTH), F32),
            pltpu.VMEM((WIDTH, WIDTH), BF16),
            pltpu.VMEM((RANK, WIDTH), F32),
            pltpu.VMEM((2 * WIN, WIDTH), BF16),
            pltpu.VMEM((4, WIN, WIDTH), BF16),
            pltpu.VMEM((WIN, WIDTH), BF16),
            pltpu.VMEM((WIN, WIDTH), BF16),
            pltpu.VMEM((4, 4, WIN, WIN), F32),
            pltpu.VMEM((4, 2 * WIN, WIDTH), BF16),
            pltpu.VMEM((16, RANK, WIDTH), F32),
            pltpu.VMEM((16, RANK, WIDTH), BF16),
            pltpu.VMEM((16, RANK, WIDTH), BF16),
            pltpu.VMEM((2, 3, 2, RANK, WIDTH), BF16),
            pltpu.VMEM((2, 3, 2, RANK, WIDTH), BF16),
            pltpu.VMEM((4, RANK, WIDTH), F32),
            pltpu.VMEM((2, 3, 16, WIDTH), BF16),
            pltpu.VMEM((2, 3, 16, WIDTH), BF16),
            pltpu.VMEM((4, HALF, WIDTH), BF16),
            pltpu.VMEM((4, HALF, WIDTH), BF16),
            pltpu.VMEM((2, LINE, RANK, 128), F32),
            pltpu.VMEM((2, LINE, RANK, 128), F32),
            pltpu.VMEM((2, 2, LINE, RANK, 128), F32),
            pltpu.VMEM((2, LINE, RANK, 128), F32),
            pltpu.VMEM((RANK, RANK), F32),
            pltpu.VMEM((RANK, RANK), F32),
            pltpu.SemaphoreType.DMA((8,)),
            pltpu.SemaphoreType.DMA((8,)),
            pltpu.SemaphoreType.DMA((22,)),
            pltpu.SemaphoreType.DMA((22,)),
            pltpu.SemaphoreType.DMA((10,)),
            pltpu.SemaphoreType.DMA((10,)),
            pltpu.SemaphoreType.DMA((6,)),
        ],
        compiler_params=pltpu.CompilerParams(
            collective_id=0, has_side_effects=True, vmem_limit_bytes=32 * 2**20
        ),
        name="main",
    )(
        basis_seed,
        window_shift,
        *(stay(a[0]) for a in (query_rows, key_rows, value_rows, cotangent)),
        stay(out_weight),
        stay(error_rows[0]),
    )
    projected, qgrad, kgrad, vgrad, update, new_error, new_basis = pl.pallas_call(
        place_kernel,
        out_shape=results,
        in_specs=[vmem] * 7,
        out_specs=(hbm,) * 7,
        scratch_shapes=[pltpu.SemaphoreType.DMA((7,))],
        compiler_params=pltpu.CompilerParams(vmem_limit_bytes=8 * 2**20),
        name="place",
    )(*parts)
    return (
        projected[None],
        qgrad[None],
        kgrad[None],
        vgrad[None],
        update,
        new_error[None],
        new_basis.T,
    )


def solution(mesh):
    return jax.shard_map(
        body,
        mesh=mesh,
        in_specs=(
            P("rep", "tok", None),
            P("rep", "tok", None),
            P("rep", "tok", None),
            P("rep", "tok", None),
            P(),
            P("rep", "tok", None),
            P("rep"),
            P(),
        ),
        out_specs=(
            P("rep", "tok", None),
            P("rep", "tok", None),
            P("rep", "tok", None),
            P("rep", "tok", None),
            P("tok", None),
            P("rep", "tok", None),
            P(),
        ),
        check_vma=False,
    )
```
